256 devices in a mesh: grp: 8 (over z), seq: 32 (over x, y, core).
Axes of the slice: x: 4, y: 4, z: 8, core: 2. Of those that a mesh axis runs over, the one named last changes fastest.
Arguments:
- query_gate: bfloat16 [8, 32, 131072], P('grp', None, 'seq'), may hold values from -6 to 6
- key_stream: bfloat16 [8, 32, 131072], P('grp', None, 'seq'), may hold values from -6 to 6
- value_stream: bfloat16 [8, 32, 131072], P('grp', None, 'seq'), may hold values from -6 to 6
- filter_taps: float32 [32, 131072], P(None, 'seq')
- skip_gain: float32 [32], replicated, may hold values from -3 to 3
- page_pool: bfloat16 [8, 32, 16, 32, 512], P('grp', 'seq'), may hold values from -6 to 6
- page_owner: int32 [8, 256], P('grp', 'seq'), may hold values from 0 to 7, as said below
- page_slot: int32 [8, 256], P('grp', 'seq'), may hold values from 0 to 15, as said below
- suffix_blocks: int32 [8], P('grp'), may hold values from 1 to 64, as said below
Outputs:
- gated_output: bfloat16 [8, 32, 131072], P('grp', None, 'seq')
The draws below stay inside these ranges and needn't reach their ends.
Inputs may be any that keep to these rules, and one draw needn't show every extreme that they name: `page_owner`: for a block b below 256 - suffix_blocks[s], entry [s, b] is the index along grp of the device holding that block's page; that device stands at index b // 8 along seq. Of one session's blocks in one range of 8 blocks, at most 2 share an owner, and some owner holds exactly 2 in every draw. Entries of later blocks are not used. `page_slot`: entry [s, b] is the block's slot in its owner's pool: session s's pages lie in slots s * 2 to s * 2 + 1, distinct among one owner's pages of one session and range. Entries of blocks at or past 256 - suffix_blocks[s] are not used. The last suffix_blocks[s] blocks of session s are fresh; the earlier ones are cached.
All inputs are finite; a program needn't handle non-finite values.
Results may differ from the reference program's by a relative error of at most 0.012.
Values may be sent and summed in bfloat16 or wider, within the bound.
No kernel may reach another device: no remote copies, remote signals or barrier semaphores. Data moves between devices by JAX's collectives and lax.ppermute only.
A program may use at most 64 MiB of HBM per device.

```python
import jax
import jax.numpy as jnp
from jax import lax

C = 32
BLK = 512
SESS = 8
SEQ_LEN = 131072
NBLK = 256
BPD = 8
CAP = 2
SLOTS = 16
N_GRP = 8
N_SEQ = 32


def layout_tables(key):
    subkeys = jax.random.split(key, 5)
    quarter = NBLK // 4
    fresh_blocks = jax.random.randint(subkeys[0], (SESS,), 1, quarter + 1)
    chosen = jax.random.permutation(subkeys[1], SESS)
    fresh_blocks = jnp.where(chosen == 0, quarter, jnp.where(chosen == 1, 1, fresh_blocks))
    range_count = NBLK // BPD
    slot_span = SESS * CAP
    favoured = jax.random.randint(subkeys[2], (SESS, range_count, 1), 0, SESS)
    position = jnp.broadcast_to(jnp.arange(slot_span, dtype=jnp.int32), (SESS, range_count, slot_span))
    owner_of = position // CAP
    jitter = jax.random.randint(subkeys[3], (SESS, range_count, slot_span), 0, 1024)
    scores = (jitter + jnp.where(owner_of == favoured, 0, 1024)) * slot_span + position
    ordering = jnp.argsort(scores, axis=-1)[:, :, :BPD]
    block_jitter = jax.random.randint(subkeys[4], (SESS, range_count, BPD), 0, 1024)
    block_scores = block_jitter * BPD + jnp.arange(BPD, dtype=jnp.int32)
    block_order = jnp.argsort(block_scores, axis=-1)
    picked = jnp.take_along_axis(ordering, block_order, axis=-1).astype(jnp.int32)
    owners = picked // CAP
    slots = jnp.arange(SESS, dtype=jnp.int32)[:, None, None] * CAP + picked % CAP
    return (fresh_blocks.astype(jnp.int32), owners.reshape(SESS, NBLK).astype(jnp.int32), slots.reshape(SESS, NBLK).astype(jnp.int32))


def draw_suffix_blocks(key, part):
    fresh_blocks, owners, slots = layout_tables(key)
    return fresh_blocks


def draw_page_owner(key, part):
    fresh_blocks, owners, slots = layout_tables(key)
    return owners


def draw_page_slot(key, part):
    fresh_blocks, owners, slots = layout_tables(key)
    return slots


def draw_filter_taps(key, part):
    key = jax.random.fold_in(key, 7)
    subkeys = jax.random.split(key, 4)
    ranking = jax.random.permutation(subkeys[0], C)
    slow_count = C // 2
    slow_flag = ranking < slow_count
    fast_rate = jnp.exp(jax.random.uniform(subkeys[1], (C,), jnp.float32, jnp.log(1.0 / 50.0), jnp.log(1.0 / 30.0)))
    slow_rate = jnp.exp(jax.random.uniform(subkeys[2], (C,), jnp.float32, jnp.log(0.1 / SEQ_LEN), jnp.log(1.0 / SEQ_LEN)))
    decay_rate = jnp.where(slow_flag, slow_rate, fast_rate)
    energy = jnp.expm1(-2.0 * decay_rate * SEQ_LEN) / jnp.expm1(-2.0 * decay_rate)
    amplitude = 1.0 / jnp.sqrt(energy)
    positions = jnp.arange(SEQ_LEN, dtype=jnp.float32)
    jitter = jax.random.normal(subkeys[3], (C, SEQ_LEN), jnp.float32)
    return amplitude[:, None] * jnp.exp(-decay_rate[:, None] * positions[None, :]) * jitter


def block_levels(stream_key, extent, cuts, low, high):
    level, own = 1.0, jax.random.fold_in(stream_key, 6)
    for dim, blocks in cuts:
        steps = jnp.exp(jax.random.uniform(jax.random.fold_in(own, dim), (blocks,), jnp.float32, low / len(cuts), high / len(cuts)))
        level = level * jnp.repeat(steps, extent[dim] // blocks).reshape([-1 if axis == dim else 1 for axis in range(len(extent))])
    return level


def centred(rng, shape, scale, limit, shards=(), kind=jnp.bfloat16):
    drawn = jax.random.normal(rng, shape, jnp.float32) * scale
    if len(shards) > 0:
        drawn = block_levels(rng, shape, shards, -0.22, 0.18) * drawn
    return jnp.clip(drawn, min=-limit, max=limit).astype(kind)


def setup_inputs(seed: int = 0) -> dict:
    key_of = jax.random.split(jax.random.key(seed), 10)
    return {
        "query_gate": centred(key_of[0], (SESS, C, SEQ_LEN), 1.0, 6.0, ((0, 8), (2, 32))),
        "key_stream": centred(key_of[1], (SESS, C, SEQ_LEN), 1.0, 6.0, ((0, 8), (2, 32))),
        "value_stream": centred(key_of[2], (SESS, C, SEQ_LEN), 1.0, 6.0, ((0, 8), (2, 32))),
        "filter_taps": draw_filter_taps(jax.random.fold_in(key_of[9], 71), 0),
        "skip_gain": centred(key_of[4], (C,), 1.0, 3.0, (), jnp.float32),
        "page_pool": centred(key_of[5], (N_GRP, N_SEQ, SLOTS, C, BLK), 1.0, 6.0, ((0, 8), (1, 32))),
        "page_owner": draw_page_owner(jax.random.fold_in(key_of[9], 71), 0),
        "page_slot": draw_page_slot(jax.random.fold_in(key_of[9], 71), 0),
        "suffix_blocks": draw_suffix_blocks(jax.random.fold_in(key_of[9], 71), 0),
    }


def reference(query_gate, key_stream, value_stream, filter_taps, skip_gain, page_pool, page_owner, page_slot, suffix_blocks):
    length_fft = 2 * SEQ_LEN
    filter_spec = jnp.fft.rfft(filter_taps, n=length_fft, axis=-1)
    block_ids = jnp.arange(NBLK).astype(jnp.int32)
    ranges = (block_ids // BPD).astype(jnp.int32)

    def one_session(items):
        query_row, key_row, value_row, owner_row, slot_row, fresh_count = items
        pages = page_pool[owner_row, ranges, slot_row]
        cached = jnp.transpose(pages, (1, 0, 2)).reshape(C, SEQ_LEN).astype(jnp.float32)
        prefix_flag = jnp.repeat(block_ids < NBLK - fresh_count, BLK, total_repeat_length=SEQ_LEN)
        fresh_input = key_row.astype(jnp.float32) * value_row.astype(jnp.float32)
        signal = jnp.where(prefix_flag[None, :], cached, fresh_input)
        spectrum = jnp.fft.rfft(signal, n=length_fft, axis=-1)
        convolved = jnp.fft.irfft(spectrum * filter_spec, n=length_fft, axis=-1)[:, :SEQ_LEN]
        gated = query_row.astype(jnp.float32) * (convolved + skip_gain[:, None] * signal)
        return gated.astype(jnp.bfloat16)

    return lax.map(one_session, (query_gate, key_stream, value_stream, page_owner, page_slot, suffix_blocks))
```

```python
import functools

import jax
import jax.numpy as jnp
import ml_dtypes
import numpy as np
from jax import lax
from jax.experimental import pallas as pl
from jax.experimental.pallas import tpu as pltpu
from jax.sharding import PartitionSpec as P

N1 = 256
N2 = 512
HALF = N2 // 2
TOTAL = N1 * N2
BF16 = jnp.bfloat16
F32 = jnp.float32


def split_table(table):
    high = table.astype(ml_dtypes.bfloat16)
    low = (table - high.astype(np.float64)).astype(ml_dtypes.bfloat16)
    return high, low


@functools.cache
def tables():
    k1 = np.arange(N1)[:, None] + 0.25
    n1 = np.arange(N1)[None, :]
    rows = np.exp(-2j * np.pi * k1 * n1 / N1)
    high, low = split_table(np.concatenate([rows.real, rows.imag], axis=0))
    first = np.concatenate([high, low], axis=0)
    twiddle = np.exp(-2j * np.pi * k1 * np.arange(N2)[None, :] / TOTAL)
    m = np.arange(HALF)[:, None]
    l = np.arange(HALF)[None, :]
    second_high, second_low = [], []
    for p in range(2):
        f = np.exp(-2j * np.pi * m * (l + 0.5 * p) / HALF)
        full = np.block([[f.real, f.imag], [-f.imag, f.real]])
        high, low = split_table(full)
        second_high.append(high)
        second_low.append(low)
    back = rows.conj().T / TOTAL
    high, low = split_table(np.concatenate([back.real, -back.imag], axis=1))
    last = np.concatenate([high, low], axis=0)
    return (
        first,
        twiddle.real.astype(np.float32),
        twiddle.imag.astype(np.float32),
        np.stack(second_high),
        np.stack(second_low),
        last,
    )


def dot(a, b):
    return jnp.dot(a, b, preferred_element_type=F32)


def dot_t(a, b):
    return lax.dot_general(a, b, (((1,), (1,)), ((), ())), preferred_element_type=F32)


def scatter_block(ref, a, block):
    for t in range(4):
        ref[t, pl.ds(a, 32, stride=8), :] = block[:, t * 128 : (t + 1) * 128]


def stage_kernel(key_ref, value_ref, taps_ref, send_ref, signal_ref, scratch_ref):
    for a in range(8):
        cols = slice(a * N2, (a + 1) * N2)
        fresh = key_ref[:, cols].astype(F32) * value_ref[:, cols].astype(F32)
        scatter_block(signal_ref, a, fresh)
        scatter_block(scratch_ref, a, taps_ref[:, cols])
    for t in range(4):
        send_ref[:, N2 + t * 128 : N2 + (t + 1) * 128] = scratch_ref[t].astype(BF16)


def select_kernel(index_ref, cached_ref, pages_ref, send_in_ref, signal_in_ref, send_ref, signal_ref):
    send_ref[:, N2:] = send_in_ref[:, N2:]
    signal_ref[...] = signal_in_ref[...]
    for a in range(8):

        @pl.when(cached_ref[a] != 0)
        def _():
            scatter_block(signal_ref, a, pages_ref[index_ref[a]].astype(F32))

    for t in range(4):
        send_ref[:, t * 128 : (t + 1) * 128] = signal_ref[t].astype(BF16)


def conv_kernel(x_ref, first_ref, cos_ref, sin_ref, high_ref, low_ref, last_ref, out_ref):
    part = dot(first_ref[...], x_ref[...])
    real = part[:N1] + part[2 * N1 : 3 * N1]
    imag = part[N1 : 2 * N1] + part[3 * N1 :]
    cosine = cos_ref[...]
    sine = sin_ref[...]
    sums, gaps = [], []
    for item in range(2):
        cols = slice(item * N2, (item + 1) * N2)
        r, i = real[:, cols], imag[:, cols]
        br = r * cosine - i * sine
        bi = r * sine + i * cosine
        sums.append(
            jnp.concatenate([br[:, :HALF] + br[:, HALF:], bi[:, :HALF] + bi[:, HALF:]], axis=1)
        )
        gaps.append(
            jnp.concatenate([br[:, :HALF] - br[:, HALF:], bi[:, :HALF] - bi[:, HALF:]], axis=1)
        )
    turned = []
    for p, pieces in enumerate((sums, gaps)):
        c = jnp.concatenate(pieces, axis=0).astype(BF16)
        spec = dot(c, high_ref[p]) + dot(c, low_ref[p])
        xr, xi = spec[:N1, :HALF], spec[:N1, HALF:]
        hr, hi = spec[N1:, :HALF], spec[N1:, HALF:]
        prod = jnp.concatenate([xr * hr - xi * hi, xr * hi + xi * hr], axis=1).astype(BF16)
        turned.append(dot_t(prod, high_ref[p]) + dot_t(prod, low_ref[p]))
    plus = turned[0] + turned[1]
    minus = turned[0] - turned[1]
    dr = jnp.concatenate([plus[:, :HALF], minus[:, :HALF]], axis=1)
    di = jnp.concatenate([plus[:, HALF:], minus[:, HALF:]], axis=1)
    er = (dr * cosine + di * sine).astype(BF16)
    ei = (di * cosine - dr * sine).astype(BF16)
    part = dot(last_ref[...], jnp.concatenate([er, ei], axis=0))
    out_ref[...] = (part[:N1] + part[N1:]).astype(BF16)


def gate_kernel(conv_ref, signal_ref, gain_ref, query_ref, out_ref, scratch_ref):
    gain = gain_ref[...]
    for t in range(4):
        conv = conv_ref[:, t * 128 : (t + 1) * 128].astype(F32)
        scratch_ref[t] = conv + gain * signal_ref[t]
    for a in range(8):
        for t in range(4):
            cols = slice(a * N2 + t * 128, a * N2 + (t + 1) * 128)
            total = scratch_ref[t, pl.ds(a, 32, stride=8), :]
            out_ref[:, cols] = (query_ref[:, cols].astype(F32) * total).astype(BF16)


def params():
    return pltpu.CompilerParams(vmem_limit_bytes=48 * 1024 * 1024)


def cost(flops, moved):
    return pl.CostEstimate(flops=flops, bytes_accessed=moved, transcendentals=0)


VMEM = pl.BlockSpec(memory_space=pltpu.VMEM)
SMEM = pl.BlockSpec(memory_space=pltpu.SMEM)


def shards(
    query_gate,
    key_stream,
    value_stream,
    filter_taps,
    skip_gain,
    page_pool,
    page_owner,
    page_slot,
    suffix_blocks,
):
    seq_index = lax.axis_index("seq")
    grp_index = lax.axis_index("grp")
    outgoing = page_pool.reshape(8, 2, 32, N2)
    arrived = lax.all_to_all(outgoing, "grp", split_axis=0, concat_axis=0, tiled=True)
    arrived = arrived.reshape(16, 32, N2)

    index = jnp.clip(page_owner[0] * 2 + page_slot[0] - grp_index * 2, 0, 15)
    block_ids = seq_index * 8 + jnp.arange(8, dtype=jnp.int32)
    cached = (block_ids < 256 - suffix_blocks[0]).astype(jnp.int32)
    gain = jnp.repeat(skip_gain, 8)[:, None]

    send, signal = pl.pallas_call(
        stage_kernel,
        out_shape=(
            jax.ShapeDtypeStruct((N1, 2 * N2), BF16),
            jax.ShapeDtypeStruct((4, N1, 128), F32),
        ),
        in_specs=[VMEM] * 3,
        out_specs=(VMEM, VMEM),
        scratch_shapes=[pltpu.VMEM((4, N1, 128), F32)],
        compiler_params=params(),
        cost_estimate=cost(1 << 18, 1 << 21),
        name="stage",
    )(key_stream[0], value_stream[0], filter_taps)

    send, signal = pl.pallas_call(
        select_kernel,
        out_shape=(
            jax.ShapeDtypeStruct((N1, 2 * N2), BF16),
            jax.ShapeDtypeStruct((4, N1, 128), F32),
        ),
        in_specs=[SMEM, SMEM, VMEM, VMEM, VMEM],
        out_specs=(VMEM, VMEM),
        compiler_params=params(),
        cost_estimate=cost(1 << 18, 1 << 21),
        name="select",
    )(index, cached, arrived, send, signal)

    columns = lax.all_to_all(
        send.reshape(32, 8, 2 * N2), "seq", split_axis=0, concat_axis=0, tiled=True
    ).reshape(N1, 2 * N2)

    convolved = pl.pallas_call(
        conv_kernel,
        out_shape=jax.ShapeDtypeStruct((N1, N2), BF16),
        in_specs=[VMEM] * 7,
        out_specs=VMEM,
        compiler_params=params(),
        cost_estimate=cost(1 << 31, 1 << 23),
        name="conv",
    )(columns, *[jnp.asarray(t) for t in tables()])

    back = lax.all_to_all(
        convolved.reshape(32, 8, N2), "seq", split_axis=0, concat_axis=0, tiled=True
    ).reshape(N1, N2)

    gated = pl.pallas_call(
        gate_kernel,
        out_shape=jax.ShapeDtypeStruct((32, 8 * N2), BF16),
        in_specs=[VMEM] * 4,
        out_specs=VMEM,
        scratch_shapes=[pltpu.VMEM((4, N1, 128), F32)],
        compiler_params=params(),
        cost_estimate=cost(1 << 18, 1 << 21),
        name="gate",
    )(back, signal, gain, query_gate[0])
    return gated[None]


def solution(mesh):
    return jax.shard_map(
        shards,
        mesh=mesh,
        in_specs=(
            P("grp", None, "seq"),
            P("grp", None, "seq"),
            P("grp", None, "seq"),
            P(None, "seq"),
            P(),
            P("grp", "seq", None, None, None),
            P("grp", "seq"),
            P("grp", "seq"),
            P("grp"),
        ),
        out_specs=P("grp", None, "seq"),
        check_vma=False,
    )
```

```python
import functools

import jax
import jax.numpy as jnp
import ml_dtypes
import numpy as np
from jax import lax
from jax.experimental import pallas as pl
from jax.experimental.pallas import tpu as pltpu
from jax.sharding import PartitionSpec as P

N1 = 256
N2 = 512
HALF = N2 // 2
TOTAL = N1 * N2
BF16 = jnp.bfloat16
F32 = jnp.float32


def split_table(table):
    high = table.astype(ml_dtypes.bfloat16)
    low = (table - high.astype(np.float64)).astype(ml_dtypes.bfloat16)
    return high, low


@functools.cache
def tables():
    k1 = np.arange(N1)[:, None] + 0.25
    n1 = np.arange(N1)[None, :]
    rows = np.exp(-2j * np.pi * k1 * n1 / N1)
    high, low = split_table(np.concatenate([rows.real, rows.imag], axis=0))
    first = np.concatenate([high, low], axis=0)
    twiddle = np.exp(-2j * np.pi * k1 * np.arange(N2)[None, :] / TOTAL)
    m = np.arange(HALF)[:, None]
    l = np.arange(HALF)[None, :]
    second_high, second_low = [], []
    for p in range(2):
        f = np.exp(-2j * np.pi * m * (l + 0.5 * p) / HALF)
        high, low = split_table(np.concatenate([f.real, f.imag], axis=1))
        second_high.append(high)
        second_low.append(low)
    back = rows.conj().T / TOTAL
    high, low = split_table(np.concatenate([back.real, -back.imag], axis=1))
    last = np.concatenate([high, low], axis=0)
    return (
        first,
        twiddle.real.astype(np.float32),
        twiddle.imag.astype(np.float32),
        np.stack(second_high),
        np.stack(second_low),
        last,
    )


def dot(a, b):
    return jnp.dot(a, b, preferred_element_type=F32)


def dot_t(a, b):
    return lax.dot_general(a, b, (((1,), (1,)), ((), ())), preferred_element_type=F32)


def scatter_block(ref, a, block):
    for t in range(4):
        ref[t, pl.ds(a, 32, stride=8), :] = block[:, t * 128 : (t + 1) * 128]


def whole_table(half):
    return jnp.concatenate(
        [half, jnp.concatenate([-half[:, HALF:], half[:, :HALF]], axis=1)], axis=0
    )


def cut_kernel(grp_ref, pool_ref, *rest):
    outs, sems = rest[:7], rest[7]
    copies = []
    for d in range(1, 8):
        slab = lax.rem(grp_ref[0] + d, 8)
        copy = pltpu.make_async_copy(pool_ref.at[slab], outs[d - 1], sems.at[d - 1])
        copy.start()
        copies.append(copy)
    for copy in copies:
        copy.wait()


def stage_kernel(key_ref, value_ref, taps_ref, send_ref, signal_ref, scratch_ref):
    for a in range(8):
        cols = slice(a * N2, (a + 1) * N2)
        fresh = key_ref[:, cols].astype(F32) * value_ref[:, cols].astype(F32)
        scatter_block(signal_ref, a, fresh)
        scatter_block(scratch_ref, a, taps_ref[:, cols])
    for t in range(4):
        send_ref[:, N2 + t * 128 : N2 + (t + 1) * 128] = scratch_ref[t].astype(BF16)


def select_kernel(row_ref, *rest):
    pages, (send_in_ref, signal_in_ref, send_ref, signal_ref) = rest[:8], rest[8:]
    send_ref[:, N2:] = send_in_ref[:, N2:]
    signal_ref[...] = signal_in_ref[...]
    for j in range(16):
        row = row_ref[j]

        @pl.when(row >= 0)
        def _():
            scatter_block(signal_ref, row, pages[j // 2][j % 2].astype(F32))

    for t in range(4):
        send_ref[:, t * 128 : (t + 1) * 128] = signal_ref[t].astype(BF16)


def conv_kernel(x_ref, first_ref, cos_ref, sin_ref, high_ref, low_ref, last_ref, out_ref):
    part = dot(first_ref[...], x_ref[...])
    real = part[:N1] + part[2 * N1 : 3 * N1]
    imag = part[N1 : 2 * N1] + part[3 * N1 :]
    cosine = cos_ref[...]
    sine = sin_ref[...]
    sums, gaps = [], []
    for item in range(2):
        cols = slice(item * N2, (item + 1) * N2)
        r, i = real[:, cols], imag[:, cols]
        br = r * cosine - i * sine
        bi = r * sine + i * cosine
        sums.append(
            jnp.concatenate([br[:, :HALF] + br[:, HALF:], bi[:, :HALF] + bi[:, HALF:]], axis=1)
        )
        gaps.append(
            jnp.concatenate([br[:, :HALF] - br[:, HALF:], bi[:, :HALF] - bi[:, HALF:]], axis=1)
        )
    turned = []
    for p, pieces in enumerate((sums, gaps)):
        c = jnp.concatenate(pieces, axis=0).astype(BF16)
        high = whole_table(high_ref[p])
        low = whole_table(low_ref[p])
        spec = dot(c, high) + dot(c, low)
        xr, xi = spec[:N1, :HALF], spec[:N1, HALF:]
        hr, hi = spec[N1:, :HALF], spec[N1:, HALF:]
        prod = jnp.concatenate([xr * hr - xi * hi, xr * hi + xi * hr], axis=1).astype(BF16)
        turned.append(dot_t(prod, high) + dot_t(prod, low))
    plus = turned[0] + turned[1]
    minus = turned[0] - turned[1]
    dr = jnp.concatenate([plus[:, :HALF], minus[:, :HALF]], axis=1)
    di = jnp.concatenate([plus[:, HALF:], minus[:, HALF:]], axis=1)
    er = (dr * cosine + di * sine).astype(BF16)
    ei = (di * cosine - dr * sine).astype(BF16)
    part = dot(last_ref[...], jnp.concatenate([er, ei], axis=0))
    out_ref[...] = (part[:N1] + part[N1:]).astype(BF16)


def gate_kernel(conv_ref, signal_ref, gain_ref, query_ref, out_ref, scratch_ref):
    gain = gain_ref[...]
    for t in range(4):
        conv = conv_ref[:, t * 128 : (t + 1) * 128].astype(F32)
        scratch_ref[t] = conv + gain * signal_ref[t]
    for a in range(8):
        for t in range(4):
            cols = slice(a * N2 + t * 128, a * N2 + (t + 1) * 128)
            total = scratch_ref[t, pl.ds(a, 32, stride=8), :]
            out_ref[:, cols] = (query_ref[:, cols].astype(F32) * total).astype(BF16)


def params():
    return pltpu.CompilerParams(vmem_limit_bytes=48 * 1024 * 1024)


def cost(flops, moved):
    return pl.CostEstimate(flops=flops, bytes_accessed=moved, transcendentals=0)


VMEM = pl.BlockSpec(memory_space=pltpu.VMEM)
SMEM = pl.BlockSpec(memory_space=pltpu.SMEM)


def shards(
    query_gate,
    key_stream,
    value_stream,
    filter_taps,
    skip_gain,
    page_pool,
    page_owner,
    page_slot,
    suffix_blocks,
):
    seq_index = lax.axis_index("seq")
    grp_index = lax.axis_index("grp")
    pool = page_pool.reshape(8, 2, 32, N2)
    parts = pl.pallas_call(
        cut_kernel,
        out_shape=[jax.ShapeDtypeStruct((2, 32, N2), BF16)] * 7,
        in_specs=[SMEM, pl.BlockSpec(memory_space=pl.ANY)],
        out_specs=[VMEM] * 7,
        scratch_shapes=[pltpu.SemaphoreType.DMA((7,))],
        compiler_params=params(),
        cost_estimate=cost(0, 1 << 20),
        name="cut",
    )(grp_index[None], pool)
    arrived = [lax.dynamic_index_in_dim(pool, grp_index, 0, keepdims=False)]
    for d in range(1, 8):
        arrived.append(lax.ppermute(parts[d - 1], "grp", [(z, (z + d) % 8) for z in range(8)]))

    block_ids = seq_index * 8 + jnp.arange(8, dtype=jnp.int32)
    cached = block_ids < 256 - suffix_blocks[0]
    index = ((grp_index - page_owner[0]) & 7) * 2 + page_slot[0] - grp_index * 2
    hits = (index[None, :] == jnp.arange(16, dtype=jnp.int32)[:, None]) & cached[None, :]
    rows = jnp.max(jnp.where(hits, jnp.arange(8, dtype=jnp.int32)[None, :], -1), axis=1)
    gain = jnp.repeat(skip_gain, 8)[:, None]

    send, signal = pl.pallas_call(
        stage_kernel,
        out_shape=(
            jax.ShapeDtypeStruct((N1, 2 * N2), BF16),
            jax.ShapeDtypeStruct((4, N1, 128), F32),
        ),
        in_specs=[VMEM] * 3,
        out_specs=(VMEM, VMEM),
        scratch_shapes=[pltpu.VMEM((4, N1, 128), F32)],
        compiler_params=params(),
        cost_estimate=cost(1 << 18, 1 << 21),
        name="stage",
    )(key_stream[0], value_stream[0], filter_taps)

    send, signal = pl.pallas_call(
        select_kernel,
        out_shape=(
            jax.ShapeDtypeStruct((N1, 2 * N2), BF16),
            jax.ShapeDtypeStruct((4, N1, 128), F32),
        ),
        in_specs=[SMEM] + [VMEM] * 10,
        out_specs=(VMEM, VMEM),
        compiler_params=params(),
        cost_estimate=cost(1 << 18, 1 << 21),
        name="select",
    )(rows, *arrived, send, signal)

    columns = lax.all_to_all(
        send.reshape(32, 8, 2 * N2), "seq", split_axis=0, concat_axis=0, tiled=True
    ).reshape(N1, 2 * N2)

    convolved = pl.pallas_call(
        conv_kernel,
        out_shape=jax.ShapeDtypeStruct((N1, N2), BF16),
        in_specs=[VMEM] * 7,
        out_specs=VMEM,
        compiler_params=params(),
        cost_estimate=cost(1 << 31, 1 << 23),
        name="conv",
    )(columns, *[jnp.asarray(t) for t in tables()])

    back = lax.all_to_all(
        convolved.reshape(32, 8, N2), "seq", split_axis=0, concat_axis=0, tiled=True
    ).reshape(N1, N2)

    gated = pl.pallas_call(
        gate_kernel,
        out_shape=jax.ShapeDtypeStruct((32, 8 * N2), BF16),
        in_specs=[VMEM] * 4,
        out_specs=VMEM,
        scratch_shapes=[pltpu.VMEM((4, N1, 128), F32)],
        compiler_params=params(),
        cost_estimate=cost(1 << 18, 1 << 21),
        name="gate",
    )(back, signal, gain, query_gate[0])
    return gated[None]


def solution(mesh):
    return jax.shard_map(
        shards,
        mesh=mesh,
        in_specs=(
            P("grp", None, "seq"),
            P("grp", None, "seq"),
            P("grp", None, "seq"),
            P(None, "seq"),
            P(),
            P("grp", "seq", None, None, None),
            P("grp", "seq"),
            P("grp", "seq"),
            P("grp"),
        ),
        out_specs=P("grp", None, "seq"),
        check_vma=False,
    )
```

```python
import functools

import jax
import jax.numpy as jnp
import ml_dtypes
import numpy as np
from jax import lax
from jax.experimental import pallas as pl
from jax.experimental.pallas import tpu as pltpu
from jax.sharding import PartitionSpec as P

N1 = 256
N2 = 512
HALF = N2 // 2
TOTAL = N1 * N2
BF16 = jnp.bfloat16
F32 = jnp.float32


def split_table(table):
    high = table.astype(ml_dtypes.bfloat16)
    low = (table - high.astype(np.float64)).astype(ml_dtypes.bfloat16)
    return high, low


@functools.cache
def tables():
    k1 = np.arange(N1)[:, None] + 0.25
    n1 = np.arange(N1)[None, :]
    rows = np.exp(-2j * np.pi * k1 * n1 / N1)
    high, low = split_table(np.concatenate([rows.real, rows.imag], axis=0))
    first = np.concatenate([high, low], axis=0)
    twiddle = np.exp(-2j * np.pi * k1 * np.arange(N2)[None, :] / TOTAL)
    m = np.arange(HALF)[:, None]
    l = np.arange(HALF)[None, :]
    second_high, second_low = [], []
    for p in range(2):
        f = np.exp(-2j * np.pi * m * (l + 0.5 * p) / HALF)
        high, low = split_table(np.concatenate([f.real, f.imag], axis=1))
        second_high.append(high)
        second_low.append(low)
    back = rows.conj().T / TOTAL
    high, low = split_table(np.concatenate([back.real, -back.imag], axis=1))
    last = np.concatenate([high, low], axis=0)
    return (
        first,
        twiddle.real.astype(np.float32),
        twiddle.imag.astype(np.float32),
        np.stack(second_high),
        np.stack(second_low),
        last,
    )


def dot(a, b):
    return jnp.dot(a, b, preferred_element_type=F32)


def dot_t(a, b):
    return lax.dot_general(a, b, (((1,), (1,)), ((), ())), preferred_element_type=F32)


def whole_table(half):
    return jnp.concatenate(
        [half, jnp.concatenate([-half[:, HALF:], half[:, :HALF]], axis=1)], axis=0
    )


def place_rows(key_row):
    rows = lax.broadcasted_iota(jnp.int32, (N1, key_row.shape[1]), 0)
    return (rows == key_row).astype(F32).astype(BF16)


def block_order(to_send):
    col = lax.broadcasted_iota(jnp.int32, (1, N1), 1)
    if to_send:
        return place_rows((col & 31) * 8 + (col >> 5))
    return place_rows((col & 7) * 32 + (col >> 3))


def fetch(sources, targets, sems):
    copies = [
        pltpu.make_async_copy(source, target, sems.at[i])
        for i, (source, target) in enumerate(zip(sources, targets))
    ]
    for copy in copies:
        copy.start()
    for copy in copies:
        copy.wait()


def cut_kernel(pool_ref, *rest):
    outs, sems = rest[:8], rest[8]
    here = lax.axis_index("grp")
    fetch([pool_ref.at[lax.rem(here + d, 8)] for d in range(8)], outs, sems)


def stage_kernel(
    owner_ref,
    slot_ref,
    suffix_ref,
    gain_ref,
    key_hbm,
    value_hbm,
    taps_hbm,
    tie_ref,
    taps_ref,
    fresh_send_ref,
    fresh_ref,
    send_key_ref,
    plain_key_ref,
    gain_rows_ref,
    key_ref,
    value_ref,
    plain_ref,
    sems,
):
    del tie_ref
    fetch([key_hbm, value_hbm, taps_hbm], [key_ref, value_ref, plain_ref], sems)
    here = lax.axis_index("grp")
    count = 256 - suffix_ref[0] - lax.axis_index("seq") * 8
    column = lax.broadcasted_iota(jnp.int32, (1, 512), 1)
    channel = column & 31
    send_key = jnp.full((1, 512), -1, jnp.int32)
    plain_key = jnp.full((1, 512), -1, jnp.int32)
    taps = []
    for a in range(8):
        page = ((here - owner_ref[0, a]) & 7) * 2 + slot_ref[0, a] - here * 2
        hit = (column >> 5) == jnp.where(a < count, page, -1)
        send_key = jnp.where(hit, channel * 8 + a, send_key)
        plain_key = jnp.where(hit, channel + a * 32, plain_key)
        cols = slice(a * N2, (a + 1) * N2)
        product = key_ref[:, cols].astype(F32) * value_ref[:, cols].astype(F32)
        fresh_ref[a * 32 : (a + 1) * 32, :] = jnp.where(a < count, 0.0, product)
        taps.append(plain_ref[:, cols])
    send_key_ref[...] = send_key
    plain_key_ref[...] = plain_key
    lane = lax.broadcasted_iota(jnp.int32, (N1, 1), 0) & 31
    gain = jnp.zeros((N1, 1), F32)
    for c in range(32):
        gain = jnp.where(lane == c, gain_ref[c], gain)
    gain_rows_ref[...] = gain
    order = block_order(True)
    taps_ref[...] = dot(order, jnp.concatenate(taps, axis=0).astype(BF16)).astype(BF16)
    fresh_send_ref[...] = dot(order, fresh_ref[...].astype(BF16)).astype(BF16)


def select_kernel(send_key_ref, key_ref, gain_ref, taps_ref, fresh_send_ref, fresh_ref, *rest):
    slabs, (send_ref, direct_ref) = rest[:8], rest[8:]
    pages = jnp.concatenate([slab[...].reshape(64, N2) for slab in slabs], axis=0)
    cached = dot(place_rows(send_key_ref[...]), pages)
    send_ref[:, :N2] = (cached + fresh_send_ref[...].astype(F32)).astype(BF16)
    send_ref[:, N2:] = taps_ref[...]
    direct_ref[...] = gain_ref[...] * (dot(place_rows(key_ref[...]), pages) + fresh_ref[...])


def conv_kernel(x_ref, first_ref, cos_ref, sin_ref, high_ref, low_ref, last_ref, out_ref):
    part = dot(first_ref[...], x_ref[...])
    real = part[:N1] + part[2 * N1 : 3 * N1]
    imag = part[N1 : 2 * N1] + part[3 * N1 :]
    cosine = cos_ref[...]
    sine = sin_ref[...]
    sums, gaps = [], []
    for item in range(2):
        cols = slice(item * N2, (item + 1) * N2)
        r, i = real[:, cols], imag[:, cols]
        br = r * cosine - i * sine
        bi = r * sine + i * cosine
        sums.append(
            jnp.concatenate([br[:, :HALF] + br[:, HALF:], bi[:, :HALF] + bi[:, HALF:]], axis=1)
        )
        gaps.append(
            jnp.concatenate([br[:, :HALF] - br[:, HALF:], bi[:, :HALF] - bi[:, HALF:]], axis=1)
        )
    turned = []
    for p, pieces in enumerate((sums, gaps)):
        c = jnp.concatenate(pieces, axis=0).astype(BF16)
        high = whole_table(high_ref[p])
        low = whole_table(low_ref[p])
        spec = dot(c, high) + dot(c, low)
        xr, xi = spec[:N1, :HALF], spec[:N1, HALF:]
        hr, hi = spec[N1:, :HALF], spec[N1:, HALF:]
        prod = jnp.concatenate([xr * hr - xi * hi, xr * hi + xi * hr], axis=1).astype(BF16)
        turned.append(dot_t(prod, high) + dot_t(prod, low))
    plus = turned[0] + turned[1]
    minus = turned[0] - turned[1]
    dr = jnp.concatenate([plus[:, :HALF], minus[:, :HALF]], axis=1)
    di = jnp.concatenate([plus[:, HALF:], minus[:, HALF:]], axis=1)
    er = (dr * cosine + di * sine).astype(BF16)
    ei = (di * cosine - dr * sine).astype(BF16)
    part = dot(last_ref[...], jnp.concatenate([er, ei], axis=0))
    out_ref[...] = (part[:N1] + part[N1:]).astype(BF16)


def gate_kernel(conv_ref, direct_ref, query_ref, out_ref):
    total = dot(block_order(False), conv_ref[...]) + direct_ref[...]
    for a in range(8):
        cols = slice(a * N2, (a + 1) * N2)
        query = query_ref[:, cols].astype(F32)
        out_ref[:, cols] = (query * total[a * 32 : (a + 1) * 32, :]).astype(BF16)


def params():
    return pltpu.CompilerParams(vmem_limit_bytes=48 * 1024 * 1024)


def in_hbm(array):
    return pltpu.with_memory_space_constraint(array, pltpu.HBM)


def cost(flops, moved):
    return pl.CostEstimate(flops=flops, bytes_accessed=moved, transcendentals=0)


VMEM = pl.BlockSpec(memory_space=pltpu.VMEM)
SMEM = pl.BlockSpec(memory_space=pltpu.SMEM)
HBM = pl.BlockSpec(memory_space=pltpu.HBM)


def shards(
    query_gate,
    key_stream,
    value_stream,
    filter_taps,
    skip_gain,
    page_pool,
    page_owner,
    page_slot,
    suffix_blocks,
):
    slabs = pl.pallas_call(
        cut_kernel,
        out_shape=[jax.ShapeDtypeStruct((2, 32, N2), BF16)] * 8,
        in_specs=[HBM],
        out_specs=[VMEM] * 8,
        scratch_shapes=[pltpu.SemaphoreType.DMA((8,))],
        compiler_params=params(),
        cost_estimate=cost(0, 1 << 20),
        name="cut",
    )(in_hbm(page_pool.reshape(8, 2, 32, N2)))
    slabs = list(slabs)
    for d in range(1, 8):
        slabs[d] = lax.ppermute(slabs[d], "grp", [(z, (z + d) % 8) for z in range(8)])

    taps, fresh_send, fresh, send_key, plain_key, gain = pl.pallas_call(
        stage_kernel,
        out_shape=(
            jax.ShapeDtypeStruct((N1, N2), BF16),
            jax.ShapeDtypeStruct((N1, N2), BF16),
            jax.ShapeDtypeStruct((N1, N2), F32),
            jax.ShapeDtypeStruct((1, 512), jnp.int32),
            jax.ShapeDtypeStruct((1, 512), jnp.int32),
            jax.ShapeDtypeStruct((N1, 1), F32),
        ),
        in_specs=[SMEM] * 4 + [HBM] * 3 + [pl.BlockSpec(memory_space=pl.ANY)],
        out_specs=(VMEM,) * 6,
        scratch_shapes=[
            pltpu.VMEM((32, 8 * N2), BF16),
            pltpu.VMEM((32, 8 * N2), BF16),
            pltpu.VMEM((32, 8 * N2), F32),
            pltpu.SemaphoreType.DMA((3,)),
        ],
        compiler_params=params(),
        cost_estimate=cost(1 << 18, 1 << 21),
        name="stage",
    )(
        page_owner,
        page_slot,
        suffix_blocks,
        skip_gain,
        in_hbm(key_stream[0]),
        in_hbm(value_stream[0]),
        in_hbm(filter_taps),
        slabs[1],
    )

    send, direct = pl.pallas_call(
        select_kernel,
        out_shape=(
            jax.ShapeDtypeStruct((N1, 2 * N2), BF16),
            jax.ShapeDtypeStruct((N1, N2), F32),
        ),
        in_specs=[VMEM] * 14,
        out_specs=(VMEM, VMEM),
        compiler_params=params(),
        cost_estimate=cost(1 << 18, 1 << 21),
        name="select",
    )(send_key, plain_key, gain, taps, fresh_send, fresh, *slabs)

    columns = lax.all_to_all(
        send.reshape(32, 8, 2 * N2), "seq", split_axis=0, concat_axis=0, tiled=True
    ).reshape(N1, 2 * N2)

    convolved = pl.pallas_call(
        conv_kernel,
        out_shape=jax.ShapeDtypeStruct((N1, N2), BF16),
        in_specs=[VMEM] * 7,
        out_specs=VMEM,
        compiler_params=params(),
        cost_estimate=cost(1 << 31, 1 << 23),
        name="conv",
    )(columns, *[jnp.asarray(t) for t in tables()])

    back = lax.all_to_all(
        convolved.reshape(32, 8, N2), "seq", split_axis=0, concat_axis=0, tiled=True
    ).reshape(N1, N2)

    gated = pl.pallas_call(
        gate_kernel,
        out_shape=jax.ShapeDtypeStruct((32, 8 * N2), BF16),
        in_specs=[VMEM] * 3,
        out_specs=VMEM,
        compiler_params=params(),
        cost_estimate=cost(1 << 18, 1 << 21),
        name="gate",
    )(back, direct, query_gate[0])
    return gated[None]


def solution(mesh):
    return jax.shard_map(
        shards,
        mesh=mesh,
        in_specs=(
            P("grp", None, "seq"),
            P("grp", None, "seq"),
            P("grp", None, "seq"),
            P(None, "seq"),
            P(),
            P("grp", "seq", None, None, None),
            P("grp", "seq"),
            P("grp", "seq"),
            P("grp"),
        ),
        out_specs=P("grp", None, "seq"),
        check_vma=False,
    )
```

```python
import functools

import jax
import jax.numpy as jnp
import ml_dtypes
import numpy as np
from jax import lax
from jax.experimental import pallas as pl
from jax.experimental.pallas import tpu as pltpu
from jax.sharding import PartitionSpec as P

N1 = 256
N2 = 512
HALF = N2 // 2
TOTAL = N1 * N2
BF16 = jnp.bfloat16
F32 = jnp.float32


def split_table(table):
    high = table.astype(ml_dtypes.bfloat16)
    low = (table - high.astype(np.float64)).astype(ml_dtypes.bfloat16)
    return high, low


@functools.cache
def tables():
    k1 = np.arange(N1)[:, None] + 0.25
    n1 = np.arange(N1)[None, :]
    rows = np.exp(-2j * np.pi * k1 * n1 / N1)
    high, low = split_table(np.concatenate([rows.real, rows.imag], axis=0))
    first = np.concatenate([high, low], axis=0)
    twiddle = np.exp(-2j * np.pi * k1 * np.arange(128)[None, :] / TOTAL)
    m = np.arange(HALF)[:, None]
    l = np.arange(HALF)[None, :]
    second_high, second_low = [], []
    for p in range(2):
        f = np.exp(-2j * np.pi * m * (l + 0.5 * p) / HALF)
        high, low = split_table(np.concatenate([f.real, f.imag], axis=1))
        second_high.append(high)
        second_low.append(low)
    back = rows.conj().T / TOTAL
    high, low = split_table(np.concatenate([back.real, -back.imag], axis=1))
    last = np.concatenate([high, low], axis=0)
    return (
        first,
        twiddle.real.astype(np.float32),
        twiddle.imag.astype(np.float32),
        np.stack(second_high),
        np.stack(second_low),
        last,
    )


def dot(a, b):
    return jnp.dot(a, b, preferred_element_type=F32)


def dot_t(a, b):
    return lax.dot_general(a, b, (((1,), (1,)), ((), ())), preferred_element_type=F32)


def whole_table(half):
    return jnp.concatenate(
        [half, jnp.concatenate([-half[:, HALF:], half[:, :HALF]], axis=1)], axis=0
    )


def place_rows(key_row):
    rows = lax.broadcasted_iota(jnp.int32, (N1, key_row.shape[1]), 0)
    return (rows == key_row).astype(F32).astype(BF16)


def send_order():
    col = lax.broadcasted_iota(jnp.int32, (1, N1), 1)
    return (col & 31) * 8 + (col >> 5)


def block_order():
    col = lax.broadcasted_iota(jnp.int32, (1, N1), 1)
    return (col & 7) * 32 + (col >> 3)


def fetch(sources, targets, sems):
    copies = [
        pltpu.make_async_copy(source, target, sems.at[i])
        for i, (source, target) in enumerate(zip(sources, targets))
    ]
    for copy in copies:
        copy.start()
    for copy in copies:
        copy.wait()


def place():
    seq = lax.axis_index("seq")
    return seq >> 3, (seq >> 1) & 3, seq & 1


def reorder(key_row, rows):
    return dot(place_rows(key_row), rows).astype(BF16)


def taps_core_kernel(taps_ref, keep_ref, send_ref):
    _, _, core = place()
    rows = jnp.concatenate([taps_ref[:, a * N2 : (a + 1) * N2] for a in range(8)], axis=0)
    col = lax.broadcasted_iota(jnp.int32, (1, N1), 1)
    channel, block = col & 31, col >> 5
    other = (channel & 1) ^ core
    key = other * 128 + ((channel >> 1) & 3) * 32 + (channel >> 3) * 8 + block
    full = reorder(key, rows.astype(BF16))
    keep_ref[...] = full[:128]
    send_ref[...] = full[128:]


def taps_y_kernel(keep_ref, came_ref, *outs):
    _, y, core = place()
    col = lax.broadcasted_iota(jnp.int32, (1, N1), 1)
    step = (((col >> 5) & 3) - y) & 3
    key = step * 64 + ((col >> 3) & 3) * 16 + ((col >> 7) ^ core) * 8 + (col & 7)
    full = reorder(key, jnp.concatenate([keep_ref[...], came_ref[...]], axis=0))
    for d in range(4):
        outs[d][...] = full[d * 64 : (d + 1) * 64]


def taps_x_kernel(*refs):
    ins, outs = refs[:4], refs[-4:]
    x, y, _ = place()
    col = lax.broadcasted_iota(jnp.int32, (1, N1), 1)
    step = (((col >> 4) & 3) - x) & 3
    key = step * 64 + ((y - (col >> 6)) & 3) * 16 + (col & 15)
    full = reorder(key, jnp.concatenate([ref[...] for ref in ins], axis=0))
    for d in range(4):
        outs[d][...] = full[d * 64 : (d + 1) * 64]


def stage_kernel(
    owner_hbm,
    slot_hbm,
    suffix_ref,
    key_hbm,
    value_hbm,
    tie_ref,
    fresh_ref,
    row_key_ref,
    owner_ref,
    slot_ref,
    key_ref,
    value_ref,
    sems,
):
    del tie_ref
    fetch(
        [owner_hbm, slot_hbm, key_hbm, value_hbm],
        [owner_ref, slot_ref, key_ref, value_ref],
        sems,
    )
    owner, slot = owner_ref[...], slot_ref[...]
    count = 256 - lax.axis_index("seq") * 8 - suffix_ref[0]
    column = lax.broadcasted_iota(jnp.int32, (1, 512), 1)
    row_key = jnp.full((1, 512), -1, jnp.int32)
    page = owner * 2 + slot - lax.axis_index("grp") * 2
    fresh = []
    for a in range(8):
        hit = ((column >> 5) == page[:, a : a + 1]) & (count > a)
        row_key = jnp.where(hit, (column & 31) * 8 + a, row_key)
        cols = slice(a * N2, (a + 1) * N2)
        product = key_ref[:, cols].astype(F32) * value_ref[:, cols].astype(F32)
        fresh.append(jnp.where(count > a, 0.0, product))
    row_key_ref[...] = row_key
    fresh_ref[...] = reorder(send_order(), jnp.concatenate(fresh, axis=0).astype(BF16))


def select_kernel(row_key_ref, fresh_ref, pages_ref, send_ref):
    cached = dot(place_rows(row_key_ref[...]), pages_ref[...])
    send_ref[...] = (cached + fresh_ref[...].astype(F32)).astype(BF16)


def twiddles(cos_ref, sin_ref):
    c, s = cos_ref[...], sin_ref[...]
    half_c, half_s = c[:, 64:65], s[:, 64:65]
    step_c, step_s = half_c * half_c - half_s * half_s, 2.0 * half_c * half_s
    cosines, sines = [c], [s]
    for _ in range(3):
        c, s = c * step_c - s * step_s, c * step_s + s * step_c
        cosines.append(c)
        sines.append(s)
    return jnp.concatenate(cosines, axis=1), jnp.concatenate(sines, axis=1)


def forward(rows, first_ref, cosine, sine, high_ref, low_ref):
    part = dot(first_ref[...], rows)
    r = part[:N1] + part[2 * N1 : 3 * N1]
    i = part[N1 : 2 * N1] + part[3 * N1 :]
    br = r * cosine - i * sine
    bi = r * sine + i * cosine
    spectra = []
    for p, sign in enumerate((1.0, -1.0)):
        cr = br[:, :HALF] + sign * br[:, HALF:]
        ci = bi[:, :HALF] + sign * bi[:, HALF:]
        c = jnp.concatenate([cr, ci], axis=1).astype(BF16)
        spectra.append(dot(c, whole_table(high_ref[p])) + dot(c, whole_table(low_ref[p])))
    return spectra


def filter_kernel(*refs):
    taps, refs = refs[:4], refs[4:]
    gain_ref, first_hbm, cos_ref, sin_ref, high_ref, low_ref, *refs = refs
    out_ref, first_ref, mine_ref, rows_ref, sems = refs
    fetch([first_hbm], [first_ref], sems)
    x, _, _ = place()
    for d in range(4):
        start = pl.multiple_of(((x - d) & 3) * 64, 64)
        rows_ref[pl.ds(start, 64), :] = taps[d][...]
    lane = lax.broadcasted_iota(jnp.int32, (1, 32), 1)
    mine = jnp.where(lane == lax.axis_index("seq"), gain_ref[...], 0.0)
    mine_ref[...] = jnp.broadcast_to(jnp.sum(mine, axis=1, keepdims=True), (1, N2))
    cosine, sine = twiddles(cos_ref, sin_ref)
    spectra = forward(rows_ref[...], first_ref, cosine, sine, high_ref, low_ref)
    for p, spec in enumerate(spectra):
        out_ref[p] = spec


def conv_kernel(x_ref, filter_ref, gain_ref, *refs):
    first_ref, cos_ref, sin_ref, high_ref, low_ref, last_hbm, out_ref, last_ref, sem = refs
    copy = pltpu.make_async_copy(last_hbm, last_ref, sem)
    copy.start()
    turned = []
    cosine, sine = twiddles(cos_ref, sin_ref)
    spectra = forward(x_ref[...], first_ref, cosine, sine, high_ref, low_ref)
    for p, spec in enumerate(spectra):
        xr, xi = spec[:, :HALF], spec[:, HALF:]
        hr, hi = filter_ref[p, :, :HALF], filter_ref[p, :, HALF:]
        prod = jnp.concatenate([xr * hr - xi * hi, xr * hi + xi * hr], axis=1).astype(BF16)
        high, low = whole_table(high_ref[p]), whole_table(low_ref[p])
        turned.append(dot_t(prod, high) + dot_t(prod, low))
    plus = turned[0] + turned[1]
    minus = turned[0] - turned[1]
    dr = jnp.concatenate([plus[:, :HALF], minus[:, :HALF]], axis=1)
    di = jnp.concatenate([plus[:, HALF:], minus[:, HALF:]], axis=1)
    er = (dr * cosine + di * sine).astype(BF16)
    ei = (di * cosine - dr * sine).astype(BF16)
    copy.wait()
    part = dot(last_ref[...], jnp.concatenate([er, ei], axis=0))
    direct = gain_ref[...] * x_ref[...].astype(F32)
    out_ref[...] = (part[:N1] + part[N1:] + direct).astype(BF16)


def gate_kernel(total_ref, query_ref, out_ref):
    total = dot(place_rows(block_order()), total_ref[...])
    for a in range(8):
        cols = slice(a * N2, (a + 1) * N2)
        query = query_ref[:, cols].astype(F32)
        out_ref[:, cols] = (query * total[a * 32 : (a + 1) * 32, :]).astype(BF16)


def params():
    return pltpu.CompilerParams(vmem_limit_bytes=24 * 1024 * 1024)


def in_hbm(array):
    return pltpu.with_memory_space_constraint(array, pltpu.HBM)


def cost(flops, moved):
    return pl.CostEstimate(flops=flops, bytes_accessed=moved, transcendentals=0)


VMEM = pl.BlockSpec(memory_space=pltpu.VMEM)
ANY = pl.BlockSpec(memory_space=pl.ANY)
HBM = pl.BlockSpec(memory_space=pltpu.HBM)
SMEM = pl.BlockSpec(memory_space=pltpu.SMEM)


def hops(dx, dy, dcore):
    pairs = []
    for x in range(4):
        for y in range(4):
            for core in range(2):
                to = (((x + dx) % 4) * 4 + (y + dy) % 4) * 2 + (core + dcore) % 2
                pairs.append(((x * 4 + y) * 2 + core, to))
    return pairs


def shards(
    query_gate,
    key_stream,
    value_stream,
    filter_taps,
    skip_gain,
    page_pool,
    page_owner,
    page_slot,
    suffix_blocks,
):
    pages = lax.all_to_all(
        page_pool.reshape(8, 2, 32, N2), "grp", split_axis=0, concat_axis=0, tiled=True
    ).reshape(512, N2)

    rows_of = lambda rows: jax.ShapeDtypeStruct((rows, N2), BF16)
    call = functools.partial(
        pl.pallas_call, compiler_params=params(), cost_estimate=cost(0, 1 << 20)
    )
    keep, other = call(
        taps_core_kernel,
        out_shape=(rows_of(128),) * 2,
        in_specs=[VMEM],
        out_specs=(VMEM,) * 2,
        name="taps_core",
    )(filter_taps)
    came = lax.ppermute(other, "seq", hops(0, 0, 1))
    along_y = call(
        taps_y_kernel,
        out_shape=(rows_of(64),) * 4,
        in_specs=[VMEM] * 2,
        out_specs=(VMEM,) * 4,
        name="taps_y",
    )(keep, came)
    moved_y = [lax.ppermute(along_y[d], "seq", hops(0, d, 0)) for d in range(1, 4)]

    fresh, row_key = call(
        stage_kernel,
        out_shape=(rows_of(N1), jax.ShapeDtypeStruct((1, 512), jnp.int32)),
        in_specs=[HBM, HBM, SMEM, HBM, HBM, ANY],
        out_specs=(VMEM,) * 2,
        scratch_shapes=[
            pltpu.VMEM((1, 8), jnp.int32),
            pltpu.VMEM((1, 8), jnp.int32),
            pltpu.VMEM((32, 8 * N2), BF16),
            pltpu.VMEM((32, 8 * N2), BF16),
            pltpu.SemaphoreType.DMA((4,)),
        ],
        name="stage",
    )(
        in_hbm(page_owner),
        in_hbm(page_slot),
        suffix_blocks,
        in_hbm(key_stream[0]),
        in_hbm(value_stream[0]),
        along_y[0],
    )

    along_x = call(
        taps_x_kernel,
        out_shape=(rows_of(64),) * 4,
        in_specs=[VMEM] * 4 + [ANY],
        out_specs=(VMEM,) * 4,
        name="taps_x",
    )(along_y[0], *moved_y, row_key)
    moved_x = [lax.ppermute(along_x[d], "seq", hops(d, 0, 0)) for d in range(1, 4)]

    send = call(
        select_kernel,
        out_shape=rows_of(N1),
        in_specs=[VMEM] * 3,
        out_specs=VMEM,
        cost_estimate=cost(1 << 34, 1 << 28),
        name="select",
    )(row_key, fresh, pages)

    columns = lax.all_to_all(
        send.reshape(32, 8, N2), "seq", split_axis=0, concat_axis=0, tiled=True
    ).reshape(N1, N2)

    first, *middle, last = [jnp.asarray(t) for t in tables()]
    spectrum, first, gain = call(
        filter_kernel,
        out_shape=(
            jax.ShapeDtypeStruct((2, N1, N2), F32),
            jax.ShapeDtypeStruct(first.shape, BF16),
            jax.ShapeDtypeStruct((1, N2), F32),
        ),
        in_specs=[VMEM] * 5 + [HBM] + [VMEM] * 4,
        out_specs=(VMEM,) * 3,
        scratch_shapes=[pltpu.VMEM((N1, N2), BF16), pltpu.SemaphoreType.DMA((1,))],
        cost_estimate=cost(1 << 34, 1 << 28),
        name="filter",
    )(along_x[0], *moved_x, skip_gain.reshape(1, 32), in_hbm(first), *middle)
    convolved = call(
        conv_kernel,
        out_shape=rows_of(N1),
        in_specs=[VMEM] * 8 + [HBM],
        out_specs=VMEM,
        scratch_shapes=[pltpu.VMEM((2 * N1, N2), BF16), pltpu.SemaphoreType.DMA],
        cost_estimate=cost(0, 1 << 23),
        name="conv",
    )(columns, spectrum, gain, first, *middle, in_hbm(last))

    back = lax.all_to_all(
        convolved.reshape(32, 8, N2), "seq", split_axis=0, concat_axis=0, tiled=True
    ).reshape(N1, N2)

    gated = call(
        gate_kernel,
        out_shape=jax.ShapeDtypeStruct((32, 8 * N2), BF16),
        in_specs=[VMEM] * 2,
        out_specs=VMEM,
        name="gate",
    )(back, query_gate[0])
    return gated[None]


def solution(mesh):
    return jax.shard_map(
        shards,
        mesh=mesh,
        in_specs=(
            P("grp", None, "seq"),
            P("grp", None, "seq"),
            P("grp", None, "seq"),
            P(None, "seq"),
            P(),
            P("grp", "seq", None, None, None),
            P("grp", "seq"),
            P("grp", "seq"),
            P("grp"),
        ),
        out_specs=P("grp", None, "seq"),
        check_vma=False,
    )
```

```python
import functools

import jax
import jax.numpy as jnp
import ml_dtypes
import numpy as np
from jax import lax
from jax.experimental import pallas as pl
from jax.experimental.pallas import tpu as pltpu
from jax.sharding import PartitionSpec as P

N1 = 256
N2 = 512
HALF = N2 // 2
TOTAL = N1 * N2
BF16 = jnp.bfloat16
F32 = jnp.float32


def split_table(table):
    high = table.astype(ml_dtypes.bfloat16)
    low = (table - high.astype(np.float64)).astype(ml_dtypes.bfloat16)
    return high, low


@functools.cache
def tables():
    k1 = np.arange(N1)[:, None] + 0.25
    n1 = np.arange(N1)[None, :]
    rows = np.exp(-2j * np.pi * k1 * n1 / N1)
    high, low = split_table(np.concatenate([rows.real, rows.imag], axis=0))
    first = np.concatenate([high, low], axis=0)
    twiddle = np.exp(-2j * np.pi * k1 * np.arange(128)[None, :] / TOTAL)
    m = np.arange(HALF)[:, None]
    l = np.arange(HALF)[None, :]
    second_high, second_low = [], []
    for p in range(2):
        f = np.exp(-2j * np.pi * m * (l + 0.5 * p) / HALF)
        high, low = split_table(np.concatenate([f.real, f.imag], axis=1))
        second_high.append(high)
        second_low.append(low)
    back = rows.conj().T / TOTAL
    high, low = split_table(np.concatenate([back.real, -back.imag], axis=1))
    last = np.concatenate([high, low], axis=0)
    return (
        first,
        twiddle.real.astype(np.float32),
        twiddle.imag.astype(np.float32),
        np.stack(second_high),
        np.stack(second_low),
        last,
    )


def dot(a, b):
    return jnp.dot(a, b, preferred_element_type=F32)


def dot_t(a, b):
    return lax.dot_general(a, b, (((1,), (1,)), ((), ())), preferred_element_type=F32)


def whole_table(half):
    return jnp.concatenate(
        [half, jnp.concatenate([-half[:, HALF:], half[:, :HALF]], axis=1)], axis=0
    )


def place_rows(key_row):
    rows = lax.broadcasted_iota(jnp.int32, (N1, key_row.shape[1]), 0)
    return (rows == key_row).astype(F32).astype(BF16)


def send_order():
    col = lax.broadcasted_iota(jnp.int32, (1, N1), 1)
    return (col & 31) * 8 + (col >> 5)


def block_order():
    col = lax.broadcasted_iota(jnp.int32, (1, N1), 1)
    return (col & 7) * 32 + (col >> 3)


def fetch(sources, targets, sems):
    copies = [
        pltpu.make_async_copy(source, target, sems.at[i])
        for i, (source, target) in enumerate(zip(sources, targets))
    ]
    for copy in copies:
        copy.start()
    for copy in copies:
        copy.wait()


def place():
    seq = lax.axis_index("seq")
    return seq >> 3, (seq >> 1) & 3, seq & 1


def reorder(key_row, rows):
    return dot(place_rows(key_row), rows).astype(BF16)


def taps_y_kernel(taps_ref, *outs):
    _, y, _ = place()
    rows = jnp.concatenate([taps_ref[:, a * N2 : (a + 1) * N2] for a in range(8)], axis=0)
    col = lax.broadcasted_iota(jnp.int32, (1, N1), 1)
    step = (((col >> 1) & 3) - y) & 3
    key = step * 64 + ((col >> 3) & 3) * 16 + (col & 1) * 8 + (col >> 5)
    full = reorder(key, rows.astype(BF16))
    for d in range(4):
        outs[d][...] = full[d * 64 : (d + 1) * 64]


def taps_x_kernel(*refs):
    ins, outs = refs[:4], refs[-4:]
    x, y, _ = place()
    col = lax.broadcasted_iota(jnp.int32, (1, N1), 1)
    step = (((col >> 4) & 3) - x) & 3
    key = step * 64 + ((col >> 3) & 1) * 32 + ((y - (col >> 6)) & 3) * 8 + (col & 7)
    full = reorder(key, jnp.concatenate([ref[...] for ref in ins], axis=0))
    for d in range(4):
        outs[d][...] = full[d * 64 : (d + 1) * 64]


def taps_core_kernel(*refs):
    ins, (keep_ref, send_ref) = refs[:4], refs[4:]
    x, _, core = place()
    col = lax.broadcasted_iota(jnp.int32, (1, N1), 1)
    other = ((col >> 5) & 1) ^ core
    key = other * 128 + ((x - (col >> 6)) & 3) * 32 + (col & 31)
    full = reorder(key, jnp.concatenate([ref[...] for ref in ins], axis=0))
    keep_ref[...] = full[:128]
    send_ref[...] = full[128:]


def stage_kernel(
    owner_hbm,
    slot_hbm,
    suffix_ref,
    key_hbm,
    value_hbm,
    tie_ref,
    fresh_ref,
    row_key_ref,
    owner_ref,
    slot_ref,
    key_ref,
    value_ref,
    sems,
):
    del tie_ref
    fetch(
        [owner_hbm, slot_hbm, key_hbm, value_hbm],
        [owner_ref, slot_ref, key_ref, value_ref],
        sems,
    )
    owner, slot = owner_ref[...], slot_ref[...]
    count = 256 - lax.axis_index("seq") * 8 - suffix_ref[0]
    column = lax.broadcasted_iota(jnp.int32, (1, 512), 1)
    row_key = jnp.full((1, 512), -1, jnp.int32)
    page = owner * 2 + slot - lax.axis_index("grp") * 2
    fresh = []
    for a in range(8):
        hit = ((column >> 5) == page[:, a : a + 1]) & (count > a)
        row_key = jnp.where(hit, (column & 31) * 8 + a, row_key)
        cols = slice(a * N2, (a + 1) * N2)
        product = key_ref[:, cols].astype(F32) * value_ref[:, cols].astype(F32)
        fresh.append(jnp.where(count > a, 0.0, product))
    row_key_ref[...] = row_key
    fresh_ref[...] = reorder(send_order(), jnp.concatenate(fresh, axis=0).astype(BF16))


def select_kernel(row_key_ref, fresh_ref, pages_ref, send_ref):
    cached = dot(place_rows(row_key_ref[...]), pages_ref[...])
    send_ref[...] = (cached + fresh_ref[...].astype(F32)).astype(BF16)


def twiddles(cos_ref, sin_ref):
    c, s = cos_ref[...], sin_ref[...]
    half_c, half_s = c[:, 64:65], s[:, 64:65]
    step_c, step_s = half_c * half_c - half_s * half_s, 2.0 * half_c * half_s
    cosines, sines = [c], [s]
    for _ in range(3):
        c, s = c * step_c - s * step_s, c * step_s + s * step_c
        cosines.append(c)
        sines.append(s)
    return jnp.concatenate(cosines, axis=1), jnp.concatenate(sines, axis=1)


def forward(rows, first_ref, cosine, sine, high_ref, low_ref):
    part = dot(first_ref[...], rows)
    r = part[:N1] + part[2 * N1 : 3 * N1]
    i = part[N1 : 2 * N1] + part[3 * N1 :]
    br = r * cosine - i * sine
    bi = r * sine + i * cosine
    spectra = []
    for p, sign in enumerate((1.0, -1.0)):
        cr = br[:, :HALF] + sign * br[:, HALF:]
        ci = bi[:, :HALF] + sign * bi[:, HALF:]
        c = jnp.concatenate([cr, ci], axis=1).astype(BF16)
        spectra.append(dot(c, whole_table(high_ref[p])) + dot(c, whole_table(low_ref[p])))
    return spectra


def filter_kernel(*refs):
    keep_ref, came_ref, gain_ref, first_hbm, cos_ref, sin_ref, high_ref, low_ref, *refs = refs
    out_ref, first_ref, mine_ref, sems = refs
    copy = pltpu.make_async_copy(first_hbm, first_ref, sems)
    copy.start()
    _, _, core = place()
    col = lax.broadcasted_iota(jnp.int32, (1, N1), 1)
    key = ((col >> 3) & 15) * 16 + ((col >> 7) ^ core) * 8 + (col & 7)
    rows = reorder(key, jnp.concatenate([keep_ref[...], came_ref[...]], axis=0))
    lane = lax.broadcasted_iota(jnp.int32, (1, 32), 1)
    mine = jnp.where(lane == lax.axis_index("seq"), gain_ref[...], 0.0)
    mine_ref[...] = jnp.broadcast_to(jnp.sum(mine, axis=1, keepdims=True), (1, N2))
    cosine, sine = twiddles(cos_ref, sin_ref)
    copy.wait()
    spectra = forward(rows, first_ref, cosine, sine, high_ref, low_ref)
    for p, spec in enumerate(spectra):
        out_ref[p] = spec


def conv_kernel(x_ref, filter_ref, gain_ref, *refs):
    first_ref, cos_ref, sin_ref, high_ref, low_ref, last_hbm, out_ref, last_ref, sem = refs
    copy = pltpu.make_async_copy(last_hbm, last_ref, sem)
    copy.start()
    turned = []
    cosine, sine = twiddles(cos_ref, sin_ref)
    spectra = forward(x_ref[...], first_ref, cosine, sine, high_ref, low_ref)
    for p, spec in enumerate(spectra):
        xr, xi = spec[:, :HALF], spec[:, HALF:]
        hr, hi = filter_ref[p, :, :HALF], filter_ref[p, :, HALF:]
        prod = jnp.concatenate([xr * hr - xi * hi, xr * hi + xi * hr], axis=1).astype(BF16)
        high, low = whole_table(high_ref[p]), whole_table(low_ref[p])
        turned.append(dot_t(prod, high) + dot_t(prod, low))
    plus = turned[0] + turned[1]
    minus = turned[0] - turned[1]
    dr = jnp.concatenate([plus[:, :HALF], minus[:, :HALF]], axis=1)
    di = jnp.concatenate([plus[:, HALF:], minus[:, HALF:]], axis=1)
    er = (dr * cosine + di * sine).astype(BF16)
    ei = (di * cosine - dr * sine).astype(BF16)
    copy.wait()
    part = dot(last_ref[...], jnp.concatenate([er, ei], axis=0))
    direct = gain_ref[...] * x_ref[...].astype(F32)
    out_ref[...] = (part[:N1] + part[N1:] + direct).astype(BF16)


def gate_kernel(total_ref, query_ref, out_ref):
    total = dot(place_rows(block_order()), total_ref[...])
    for a in range(8):
        cols = slice(a * N2, (a + 1) * N2)
        query = query_ref[:, cols].astype(F32)
        out_ref[:, cols] = (query * total[a * 32 : (a + 1) * 32, :]).astype(BF16)


def params():
    return pltpu.CompilerParams(vmem_limit_bytes=24 * 1024 * 1024)


def in_hbm(array):
    return pltpu.with_memory_space_constraint(array, pltpu.HBM)


def cost(flops, moved):
    return pl.CostEstimate(flops=flops, bytes_accessed=moved, transcendentals=0)


VMEM = pl.BlockSpec(memory_space=pltpu.VMEM)
ANY = pl.BlockSpec(memory_space=pl.ANY)
HBM = pl.BlockSpec(memory_space=pltpu.HBM)
SMEM = pl.BlockSpec(memory_space=pltpu.SMEM)


def hops(dx, dy, dcore):
    pairs = []
    for x in range(4):
        for y in range(4):
            for core in range(2):
                to = (((x + dx) % 4) * 4 + (y + dy) % 4) * 2 + (core + dcore) % 2
                pairs.append(((x * 4 + y) * 2 + core, to))
    return pairs


def shards(
    query_gate,
    key_stream,
    value_stream,
    filter_taps,
    skip_gain,
    page_pool,
    page_owner,
    page_slot,
    suffix_blocks,
):
    pages = lax.all_to_all(
        page_pool.reshape(8, 2, 32, N2), "grp", split_axis=0, concat_axis=0, tiled=True
    ).reshape(512, N2)

    rows_of = lambda rows: jax.ShapeDtypeStruct((rows, N2), BF16)
    call = functools.partial(
        pl.pallas_call, compiler_params=params(), cost_estimate=cost(0, 1 << 20)
    )
    along_y = call(
        taps_y_kernel,
        out_shape=(rows_of(64),) * 4,
        in_specs=[VMEM],
        out_specs=(VMEM,) * 4,
        name="taps_y",
    )(filter_taps)
    moved_y = [lax.ppermute(along_y[d], "seq", hops(0, d, 0)) for d in range(1, 4)]

    fresh, row_key = call(
        stage_kernel,
        out_shape=(rows_of(N1), jax.ShapeDtypeStruct((1, 512), jnp.int32)),
        in_specs=[HBM, HBM, SMEM, HBM, HBM, ANY],
        out_specs=(VMEM,) * 2,
        scratch_shapes=[
            pltpu.VMEM((1, 8), jnp.int32),
            pltpu.VMEM((1, 8), jnp.int32),
            pltpu.VMEM((32, 8 * N2), BF16),
            pltpu.VMEM((32, 8 * N2), BF16),
            pltpu.SemaphoreType.DMA((4,)),
        ],
        name="stage",
    )(
        in_hbm(page_owner),
        in_hbm(page_slot),
        suffix_blocks,
        in_hbm(key_stream[0]),
        in_hbm(value_stream[0]),
        along_y[0],
    )

    along_x = call(
        taps_x_kernel,
        out_shape=(rows_of(64),) * 4,
        in_specs=[VMEM] * 4 + [ANY],
        out_specs=(VMEM,) * 4,
        name="taps_x",
    )(along_y[0], *moved_y, row_key)
    moved_x = [lax.ppermute(along_x[d], "seq", hops(d, 0, 0)) for d in range(1, 4)]

    keep, other = call(
        taps_core_kernel,
        out_shape=(rows_of(128),) * 2,
        in_specs=[VMEM] * 4,
        out_specs=(VMEM,) * 2,
        cost_estimate=cost(1 << 34, 1 << 28),
        name="taps_core",
    )(along_x[0], *moved_x)
    came = lax.ppermute(other, "seq", hops(0, 0, 1))

    send = call(
        select_kernel,
        out_shape=rows_of(N1),
        in_specs=[VMEM] * 3,
        out_specs=VMEM,
        cost_estimate=cost(1 << 34, 1 << 28),
        name="select",
    )(row_key, fresh, pages)

    columns = lax.all_to_all(
        send.reshape(32, 8, N2), "seq", split_axis=0, concat_axis=0, tiled=True
    ).reshape(N1, N2)

    first, *middle, last = [jnp.asarray(t) for t in tables()]
    spectrum, first, gain = call(
        filter_kernel,
        out_shape=(
            jax.ShapeDtypeStruct((2, N1, N2), F32),
            jax.ShapeDtypeStruct(first.shape, BF16),
            jax.ShapeDtypeStruct((1, N2), F32),
        ),
        in_specs=[VMEM] * 3 + [HBM] + [VMEM] * 4,
        out_specs=(VMEM,) * 3,
        scratch_shapes=[pltpu.SemaphoreType.DMA],
        cost_estimate=cost(1 << 28, 1 << 28),
        name="filter",
    )(keep, came, skip_gain.reshape(1, 32), in_hbm(first), *middle)
    convolved = call(
        conv_kernel,
        out_shape=rows_of(N1),
        in_specs=[VMEM] * 8 + [HBM],
        out_specs=VMEM,
        scratch_shapes=[pltpu.VMEM((2 * N1, N2), BF16), pltpu.SemaphoreType.DMA],
        cost_estimate=cost(0, 1 << 23),
        name="conv",
    )(columns, spectrum, gain, first, *middle, in_hbm(last))

    back = lax.all_to_all(
        convolved.reshape(32, 8, N2), "seq", split_axis=0, concat_axis=0, tiled=True
    ).reshape(N1, N2)

    gated = call(
        gate_kernel,
        out_shape=jax.ShapeDtypeStruct((32, 8 * N2), BF16),
        in_specs=[VMEM] * 2,
        out_specs=VMEM,
        name="gate",
    )(back, query_gate[0])
    return gated[None]


def solution(mesh):
    return jax.shard_map(
        shards,
        mesh=mesh,
        in_specs=(
            P("grp", None, "seq"),
            P("grp", None, "seq"),
            P("grp", None, "seq"),
            P(None, "seq"),
            P(),
            P("grp", "seq", None, None, None),
            P("grp", "seq"),
            P("grp", "seq"),
            P("grp"),
        ),
        out_specs=P("grp", None, "seq"),
        check_vma=False,
    )
```

```python
import functools

import jax
import jax.numpy as jnp
import ml_dtypes
import numpy as np
from jax import lax
from jax.experimental import pallas as pl
from jax.experimental.pallas import tpu as pltpu
from jax.sharding import PartitionSpec as P

N1 = 256
N2 = 512
HALF = N2 // 2
TOTAL = N1 * N2
RANKS = (4, 0, 5, 1, 6, 2, 7, 3)
BF16 = jnp.bfloat16
F32 = jnp.float32


def split_table(table):
    high = table.astype(ml_dtypes.bfloat16)
    low = (table - high.astype(np.float64)).astype(ml_dtypes.bfloat16)
    return high, low


@functools.cache
def tables():
    k1 = np.arange(N1)[:, None] + 0.25
    n1 = np.arange(N1)[None, :]
    rows = np.exp(-2j * np.pi * k1 * n1 / N1)
    high, low = split_table(np.concatenate([rows.real, rows.imag], axis=0))
    first = np.concatenate([high, low], axis=0)
    twiddle = np.exp(-2j * np.pi * k1 * np.arange(128)[None, :] / TOTAL)
    m = np.arange(HALF)[:, None]
    l = np.arange(HALF)[None, :]
    second_high, second_low = [], []
    for p in range(2):
        f = np.exp(-2j * np.pi * m * (l + 0.5 * p) / HALF)
        high, low = split_table(np.concatenate([f.real, f.imag], axis=1))
        second_high.append(high)
        second_low.append(low)
    back = rows.conj().T / TOTAL
    high, low = split_table(np.concatenate([back.real, -back.imag], axis=1))
    last = np.concatenate([high, low], axis=0)
    return (
        first,
        twiddle.real.astype(np.float32),
        twiddle.imag.astype(np.float32),
        np.stack(second_high),
        np.stack(second_low),
        last,
    )


def dot(a, b):
    return jnp.dot(a, b, preferred_element_type=F32)


def dot_t(a, b):
    return lax.dot_general(a, b, (((1,), (1,)), ((), ())), preferred_element_type=F32)


def whole_table(half):
    return jnp.concatenate(
        [half, jnp.concatenate([-half[:, HALF:], half[:, :HALF]], axis=1)], axis=0
    )


def place_rows(key_row):
    rows = lax.broadcasted_iota(jnp.int32, (N1, key_row.shape[1]), 0)
    return (rows == key_row).astype(F32).astype(BF16)


def send_order():
    col = lax.broadcasted_iota(jnp.int32, (1, N1), 1)
    return (col & 31) * 8 + (col >> 5)


def block_order():
    col = lax.broadcasted_iota(jnp.int32, (1, N1), 1)
    return (col & 7) * 32 + (col >> 3)


def fetch(sources, targets, sems):
    copies = [
        pltpu.make_async_copy(source, target, sems.at[i])
        for i, (source, target) in enumerate(zip(sources, targets))
    ]
    for copy in copies:
        copy.start()
    for copy in copies:
        copy.wait()


def place():
    seq = lax.axis_index("seq")
    return seq >> 3, (seq >> 1) & 3, seq & 1


def reorder(key_row, rows):
    return dot(place_rows(key_row), rows).astype(BF16)


def slabs_kernel(pool_ref, out_ref, held_ref, in_sems, out_sems):
    reads = [
        pltpu.make_async_copy(pool_ref.at[z], held_ref.at[r], in_sems.at[r])
        for r, z in enumerate(RANKS)
    ]
    writes = [
        pltpu.make_async_copy(held_ref.at[r], out_ref.at[r], out_sems.at[r]) for r in range(8)
    ]
    for read in reads:
        read.start()
    for read, write in zip(reads, writes):
        read.wait()
        write.start()
    for write in writes:
        write.wait()


def taps_y_kernel(taps_ref, *outs):
    _, y, _ = place()
    rows = jnp.concatenate([taps_ref[:, a * N2 : (a + 1) * N2] for a in range(8)], axis=0)
    col = lax.broadcasted_iota(jnp.int32, (1, N1), 1)
    step = (((col >> 1) & 3) - y) & 3
    key = step * 64 + ((col >> 3) & 3) * 16 + (col & 1) * 8 + (col >> 5)
    full = reorder(key, rows.astype(BF16))
    for d in range(4):
        outs[d][...] = full[d * 64 : (d + 1) * 64]


def taps_x_kernel(*refs):
    ins, outs = refs[:4], refs[-4:]
    x, y, _ = place()
    col = lax.broadcasted_iota(jnp.int32, (1, N1), 1)
    step = (((col >> 4) & 3) - x) & 3
    key = step * 64 + ((col >> 3) & 1) * 32 + ((y - (col >> 6)) & 3) * 8 + (col & 7)
    full = reorder(key, jnp.concatenate([ref[...] for ref in ins], axis=0))
    for d in range(4):
        outs[d][...] = full[d * 64 : (d + 1) * 64]


def taps_core_kernel(*refs):
    ins, (keep_ref, send_ref) = refs[:4], refs[4:]
    x, _, core = place()
    col = lax.broadcasted_iota(jnp.int32, (1, N1), 1)
    other = ((col >> 5) & 1) ^ core
    key = other * 128 + ((x - (col >> 6)) & 3) * 32 + (col & 31)
    full = reorder(key, jnp.concatenate([ref[...] for ref in ins], axis=0))
    keep_ref[...] = full[:128]
    send_ref[...] = full[128:]


def stage_kernel(
    owner_hbm,
    slot_hbm,
    suffix_ref,
    key_hbm,
    value_hbm,
    tie_ref,
    fresh_ref,
    row_key_ref,
    owner_ref,
    slot_ref,
    key_ref,
    value_ref,
    sems,
):
    del tie_ref
    fetch(
        [owner_hbm, slot_hbm, key_hbm, value_hbm],
        [owner_ref, slot_ref, key_ref, value_ref],
        sems,
    )
    owner, slot = owner_ref[...], slot_ref[...]
    count = 256 - lax.axis_index("seq") * 8 - suffix_ref[0]
    column = lax.broadcasted_iota(jnp.int32, (1, 512), 1)
    row_key = jnp.full((1, 512), -1, jnp.int32)
    rank = sum(jnp.where(owner == z, r, 0) for r, z in enumerate(RANKS))
    page = rank * 2 + slot - lax.axis_index("grp") * 2
    fresh = []
    for a in range(8):
        hit = ((column >> 5) == page[:, a : a + 1]) & (count > a)
        row_key = jnp.where(hit, (column & 31) * 8 + a, row_key)
        cols = slice(a * N2, (a + 1) * N2)
        product = key_ref[:, cols].astype(F32) * value_ref[:, cols].astype(F32)
        fresh.append(jnp.where(count > a, 0.0, product))
    row_key_ref[...] = row_key
    fresh_ref[...] = reorder(send_order(), jnp.concatenate(fresh, axis=0).astype(BF16))


def select_kernel(row_key_ref, fresh_ref, pages_ref, send_ref):
    cached = dot(place_rows(row_key_ref[...]), pages_ref[...])
    send_ref[...] = (cached + fresh_ref[...].astype(F32)).astype(BF16)


def twiddles(cos_ref, sin_ref):
    c, s = cos_ref[...], sin_ref[...]
    half_c, half_s = c[:, 64:65], s[:, 64:65]
    step_c, step_s = half_c * half_c - half_s * half_s, 2.0 * half_c * half_s
    cosines, sines = [c], [s]
    for _ in range(3):
        c, s = c * step_c - s * step_s, c * step_s + s * step_c
        cosines.append(c)
        sines.append(s)
    return jnp.concatenate(cosines, axis=1), jnp.concatenate(sines, axis=1)


def forward(rows, first_ref, cosine, sine, high_ref, low_ref):
    part = dot(first_ref[...], rows)
    r = part[:N1] + part[2 * N1 : 3 * N1]
    i = part[N1 : 2 * N1] + part[3 * N1 :]
    br = r * cosine - i * sine
    bi = r * sine + i * cosine
    spectra = []
    for p, sign in enumerate((1.0, -1.0)):
        cr = br[:, :HALF] + sign * br[:, HALF:]
        ci = bi[:, :HALF] + sign * bi[:, HALF:]
        c = jnp.concatenate([cr, ci], axis=1).astype(BF16)
        spectra.append(dot(c, whole_table(high_ref[p])) + dot(c, whole_table(low_ref[p])))
    return spectra


def filter_kernel(*refs):
    keep_ref, came_ref, gain_ref, first_hbm, cos_ref, sin_ref, high_ref, low_ref, *refs = refs
    out_ref, first_ref, mine_ref, sems = refs
    copy = pltpu.make_async_copy(first_hbm, first_ref, sems)
    copy.start()
    _, _, core = place()
    col = lax.broadcasted_iota(jnp.int32, (1, N1), 1)
    key = ((col >> 3) & 15) * 16 + ((col >> 7) ^ core) * 8 + (col & 7)
    rows = reorder(key, jnp.concatenate([keep_ref[...], came_ref[...]], axis=0))
    lane = lax.broadcasted_iota(jnp.int32, (1, 32), 1)
    mine = jnp.where(lane == lax.axis_index("seq"), gain_ref[...], 0.0)
    mine_ref[...] = jnp.broadcast_to(jnp.sum(mine, axis=1, keepdims=True), (1, N2))
    cosine, sine = twiddles(cos_ref, sin_ref)
    copy.wait()
    spectra = forward(rows, first_ref, cosine, sine, high_ref, low_ref)
    for p, spec in enumerate(spectra):
        out_ref[p] = spec


def conv_kernel(x_ref, filter_ref, gain_ref, *refs):
    first_ref, cos_ref, sin_ref, high_ref, low_ref, last_hbm, out_ref, last_ref, sem = refs
    copy = pltpu.make_async_copy(last_hbm, last_ref, sem)
    copy.start()
    turned = []
    cosine, sine = twiddles(cos_ref, sin_ref)
    spectra = forward(x_ref[...], first_ref, cosine, sine, high_ref, low_ref)
    for p, spec in enumerate(spectra):
        xr, xi = spec[:, :HALF], spec[:, HALF:]
        hr, hi = filter_ref[p, :, :HALF], filter_ref[p, :, HALF:]
        prod = jnp.concatenate([xr * hr - xi * hi, xr * hi + xi * hr], axis=1).astype(BF16)
        high, low = whole_table(high_ref[p]), whole_table(low_ref[p])
        turned.append(dot_t(prod, high) + dot_t(prod, low))
    plus = turned[0] + turned[1]
    minus = turned[0] - turned[1]
    dr = jnp.concatenate([plus[:, :HALF], minus[:, :HALF]], axis=1)
    di = jnp.concatenate([plus[:, HALF:], minus[:, HALF:]], axis=1)
    er = (dr * cosine + di * sine).astype(BF16)
    ei = (di * cosine - dr * sine).astype(BF16)
    copy.wait()
    part = dot(last_ref[...], jnp.concatenate([er, ei], axis=0))
    direct = gain_ref[...] * x_ref[...].astype(F32)
    out_ref[...] = (part[:N1] + part[N1:] + direct).astype(BF16)


def gate_kernel(total_ref, query_ref, out_ref):
    total = dot(place_rows(block_order()), total_ref[...])
    for a in range(8):
        cols = slice(a * N2, (a + 1) * N2)
        query = query_ref[:, cols].astype(F32)
        out_ref[:, cols] = (query * total[a * 32 : (a + 1) * 32, :]).astype(BF16)


def params():
    return pltpu.CompilerParams(vmem_limit_bytes=24 * 1024 * 1024)


def in_hbm(array):
    return pltpu.with_memory_space_constraint(array, pltpu.HBM)


def cost(flops, moved):
    return pl.CostEstimate(flops=flops, bytes_accessed=moved, transcendentals=0)


VMEM = pl.BlockSpec(memory_space=pltpu.VMEM)
ANY = pl.BlockSpec(memory_space=pl.ANY)
HBM = pl.BlockSpec(memory_space=pltpu.HBM)
SMEM = pl.BlockSpec(memory_space=pltpu.SMEM)


def hops(dx, dy, dcore):
    pairs = []
    for x in range(4):
        for y in range(4):
            for core in range(2):
                to = (((x + dx) % 4) * 4 + (y + dy) % 4) * 2 + (core + dcore) % 2
                pairs.append(((x * 4 + y) * 2 + core, to))
    return pairs


def shards(
    query_gate,
    key_stream,
    value_stream,
    filter_taps,
    skip_gain,
    page_pool,
    page_owner,
    page_slot,
    suffix_blocks,
):
    rows_of = lambda rows: jax.ShapeDtypeStruct((rows, N2), BF16)
    call = functools.partial(
        pl.pallas_call, compiler_params=params(), cost_estimate=cost(0, 1 << 20)
    )
    slabs = call(
        slabs_kernel,
        out_shape=pltpu.HBM((8, 2, 32, N2), BF16),
        in_specs=[HBM],
        out_specs=HBM,
        scratch_shapes=[
            pltpu.VMEM((8, 2, 32, N2), BF16),
            pltpu.SemaphoreType.DMA((8,)),
            pltpu.SemaphoreType.DMA((8,)),
        ],
        name="slabs",
    )(in_hbm(page_pool.reshape(8, 2, 32, N2)))
    pages = lax.all_to_all(
        slabs, "grp", split_axis=0, concat_axis=0, axis_index_groups=[RANKS], tiled=True
    ).reshape(512, N2)

    along_y = call(
        taps_y_kernel,
        out_shape=(rows_of(64),) * 4,
        in_specs=[VMEM],
        out_specs=(VMEM,) * 4,
        name="taps_y",
    )(filter_taps)
    moved_y = [lax.ppermute(along_y[d], "seq", hops(0, d, 0)) for d in range(1, 4)]

    fresh, row_key = call(
        stage_kernel,
        out_shape=(rows_of(N1), jax.ShapeDtypeStruct((1, 512), jnp.int32)),
        in_specs=[HBM, HBM, SMEM, HBM, HBM, ANY],
        out_specs=(VMEM,) * 2,
        scratch_shapes=[
            pltpu.VMEM((1, 8), jnp.int32),
            pltpu.VMEM((1, 8), jnp.int32),
            pltpu.VMEM((32, 8 * N2), BF16),
            pltpu.VMEM((32, 8 * N2), BF16),
            pltpu.SemaphoreType.DMA((4,)),
        ],
        name="stage",
    )(
        in_hbm(page_owner),
        in_hbm(page_slot),
        suffix_blocks,
        in_hbm(key_stream[0]),
        in_hbm(value_stream[0]),
        along_y[0],
    )

    along_x = call(
        taps_x_kernel,
        out_shape=(rows_of(64),) * 4,
        in_specs=[VMEM] * 4 + [ANY],
        out_specs=(VMEM,) * 4,
        name="taps_x",
    )(along_y[0], *moved_y, row_key)
    moved_x = [lax.ppermute(along_x[d], "seq", hops(d, 0, 0)) for d in range(1, 4)]

    keep, other = call(
        taps_core_kernel,
        out_shape=(rows_of(128),) * 2,
        in_specs=[VMEM] * 4,
        out_specs=(VMEM,) * 2,
        cost_estimate=cost(1 << 34, 1 << 28),
        name="taps_core",
    )(along_x[0], *moved_x)
    came = lax.ppermute(other, "seq", hops(0, 0, 1))

    send = call(
        select_kernel,
        out_shape=rows_of(N1),
        in_specs=[VMEM] * 3,
        out_specs=VMEM,
        cost_estimate=cost(1 << 34, 1 << 28),
        name="select",
    )(row_key, fresh, pages)

    columns = lax.all_to_all(
        send.reshape(32, 8, N2), "seq", split_axis=0, concat_axis=0, tiled=True
    ).reshape(N1, N2)

    first, *middle, last = [jnp.asarray(t) for t in tables()]
    spectrum, first, gain = call(
        filter_kernel,
        out_shape=(
            jax.ShapeDtypeStruct((2, N1, N2), F32),
            jax.ShapeDtypeStruct(first.shape, BF16),
            jax.ShapeDtypeStruct((1, N2), F32),
        ),
        in_specs=[VMEM] * 3 + [HBM] + [VMEM] * 4,
        out_specs=(VMEM,) * 3,
        scratch_shapes=[pltpu.SemaphoreType.DMA],
        cost_estimate=cost(1 << 28, 1 << 28),
        name="filter",
    )(keep, came, skip_gain.reshape(1, 32), in_hbm(first), *middle)
    convolved = call(
        conv_kernel,
        out_shape=rows_of(N1),
        in_specs=[VMEM] * 8 + [HBM],
        out_specs=VMEM,
        scratch_shapes=[pltpu.VMEM((2 * N1, N2), BF16), pltpu.SemaphoreType.DMA],
        cost_estimate=cost(0, 1 << 23),
        name="conv",
    )(columns, spectrum, gain, first, *middle, in_hbm(last))

    back = lax.all_to_all(
        convolved.reshape(32, 8, N2), "seq", split_axis=0, concat_axis=0, tiled=True
    ).reshape(N1, N2)

    gated = call(
        gate_kernel,
        out_shape=jax.ShapeDtypeStruct((32, 8 * N2), BF16),
        in_specs=[VMEM] * 2,
        out_specs=VMEM,
        name="gate",
    )(back, query_gate[0])
    return gated[None]


def solution(mesh):
    return jax.shard_map(
        shards,
        mesh=mesh,
        in_specs=(
            P("grp", None, "seq"),
            P("grp", None, "seq"),
            P("grp", None, "seq"),
            P(None, "seq"),
            P(),
            P("grp", "seq", None, None, None),
            P("grp", "seq"),
            P("grp", "seq"),
            P("grp"),
        ),
        out_specs=P("grp", None, "seq"),
        check_vma=False,
    )
```

```python
import functools

import jax
import jax.numpy as jnp
import ml_dtypes
import numpy as np
from jax import lax
from jax.experimental import pallas as pl
from jax.experimental.pallas import tpu as pltpu
from jax.sharding import PartitionSpec as P

N1 = 256
N2 = 512
HALF = N2 // 2
TOTAL = N1 * N2
RANKS = (4, 0, 5, 1, 6, 2, 7, 3)
BF16 = jnp.bfloat16
F32 = jnp.float32


def split_table(table):
    high = table.astype(ml_dtypes.bfloat16)
    low = (table - high.astype(np.float64)).astype(ml_dtypes.bfloat16)
    return high, low


@functools.cache
def tables():
    k1 = np.arange(N1)[:, None] + 0.25
    n1 = np.arange(N1)[None, :]
    rows = np.exp(-2j * np.pi * k1 * n1 / N1)
    high, low = split_table(np.concatenate([rows.real, rows.imag], axis=0))
    first = np.concatenate([high, low], axis=0)
    twiddle = np.exp(-2j * np.pi * k1 * np.arange(128)[None, :] / TOTAL)
    m = np.arange(HALF)[:, None]
    l = np.arange(HALF)[None, :]
    second_high, second_low = [], []
    for p in range(2):
        f = np.exp(-2j * np.pi * m * (l + 0.5 * p) / HALF)
        high, low = split_table(np.concatenate([f.real, f.imag], axis=1))
        second_high.append(high)
        second_low.append(low)
    back = rows.conj().T / TOTAL
    last, _ = split_table(np.concatenate([back.real, -back.imag], axis=1))
    return (
        first,
        twiddle.real.astype(np.float32),
        twiddle.imag.astype(np.float32),
        np.stack(second_high),
        np.stack(second_low),
        last,
    )


def dot(a, b):
    return jnp.dot(a, b, preferred_element_type=F32)


def dot_t(a, b):
    return lax.dot_general(a, b, (((1,), (1,)), ((), ())), preferred_element_type=F32)


def whole_table(half):
    return jnp.concatenate(
        [half, jnp.concatenate([-half[:, HALF:], half[:, :HALF]], axis=1)], axis=0
    )


def place_rows(key_row):
    rows = lax.broadcasted_iota(jnp.int32, (N1, key_row.shape[1]), 0)
    return (rows == key_row).astype(F32).astype(BF16)


def send_order():
    col = lax.broadcasted_iota(jnp.int32, (1, N1), 1)
    return (col & 31) * 8 + (col >> 5)


def block_order():
    col = lax.broadcasted_iota(jnp.int32, (1, N1), 1)
    return (col & 7) * 32 + (col >> 3)


def fetch(sources, targets, sems):
    copies = [
        pltpu.make_async_copy(source, target, sems.at[i])
        for i, (source, target) in enumerate(zip(sources, targets))
    ]
    for copy in copies:
        copy.start()
    for copy in copies:
        copy.wait()


def place():
    seq = lax.axis_index("seq")
    return seq >> 3, (seq >> 1) & 3, seq & 1


def reorder(key_row, rows):
    return dot(place_rows(key_row), rows).astype(BF16)


def slabs_kernel(pool_ref, taps_hbm, out_ref, *refs):
    outs, (held_ref, taps_ref, in_sems, out_sems, sem) = refs[:4], refs[4:]
    reads = [
        pltpu.make_async_copy(pool_ref.at[z], held_ref.at[r], in_sems.at[r])
        for r, z in enumerate(RANKS)
    ]
    writes = [
        pltpu.make_async_copy(held_ref.at[r], out_ref.at[r], out_sems.at[r]) for r in range(8)
    ]
    taps_read = pltpu.make_async_copy(taps_hbm, taps_ref, sem)
    for read in reads:
        read.start()
    taps_read.start()
    for read, write in zip(reads, writes):
        read.wait()
        write.start()
    taps_read.wait()
    _, y, _ = place()
    rows = jnp.concatenate([taps_ref[:, a * N2 : (a + 1) * N2] for a in range(8)], axis=0)
    col = lax.broadcasted_iota(jnp.int32, (1, N1), 1)
    step = (((col >> 1) & 3) - y) & 3
    key = step * 64 + ((col >> 3) & 3) * 16 + (col & 1) * 8 + (col >> 5)
    full = reorder(key, rows.astype(BF16))
    for d in range(4):
        outs[d][...] = full[d * 64 : (d + 1) * 64]
    for write in writes:
        write.wait()


def taps_x_kernel(*refs):
    ins, outs = refs[:4], refs[-4:]
    x, y, _ = place()
    col = lax.broadcasted_iota(jnp.int32, (1, N1), 1)
    step = (((col >> 4) & 3) - x) & 3
    key = step * 64 + ((col >> 3) & 1) * 32 + ((y - (col >> 6)) & 3) * 8 + (col & 7)
    full = reorder(key, jnp.concatenate([ref[...] for ref in ins], axis=0))
    for d in range(4):
        outs[d][...] = full[d * 64 : (d + 1) * 64]


def taps_core_kernel(*refs):
    ins, (keep_ref, send_ref) = refs[:4], refs[4:]
    x, _, core = place()
    col = lax.broadcasted_iota(jnp.int32, (1, N1), 1)
    other = ((col >> 5) & 1) ^ core
    key = other * 128 + ((x - (col >> 6)) & 3) * 32 + (col & 31)
    full = reorder(key, jnp.concatenate([ref[...] for ref in ins], axis=0))
    keep_ref[...] = full[:128]
    send_ref[...] = full[128:]


def stage_kernel(
    owner_hbm,
    slot_hbm,
    suffix_ref,
    key_hbm,
    value_hbm,
    tie_ref,
    fresh_ref,
    row_key_ref,
    owner_ref,
    slot_ref,
    key_ref,
    value_ref,
    sems,
):
    del tie_ref
    fetch(
        [owner_hbm, slot_hbm, key_hbm, value_hbm],
        [owner_ref, slot_ref, key_ref, value_ref],
        sems,
    )
    owner, slot = owner_ref[...], slot_ref[...]
    count = 256 - lax.axis_index("seq") * 8 - suffix_ref[0]
    column = lax.broadcasted_iota(jnp.int32, (1, 512), 1)
    row_key = jnp.full((1, 512), -1, jnp.int32)
    rank = sum(jnp.where(owner == z, r, 0) for r, z in enumerate(RANKS))
    page = rank * 2 + slot - lax.axis_index("grp") * 2
    fresh = []
    for a in range(8):
        hit = ((column >> 5) == page[:, a : a + 1]) & (count > a)
        row_key = jnp.where(hit, (column & 31) * 8 + a, row_key)
        cols = slice(a * N2, (a + 1) * N2)
        product = key_ref[:, cols].astype(F32) * value_ref[:, cols].astype(F32)
        fresh.append(jnp.where(count > a, 0.0, product))
    row_key_ref[...] = row_key
    fresh_ref[...] = reorder(send_order(), jnp.concatenate(fresh, axis=0).astype(BF16))


def select_kernel(row_key_ref, fresh_ref, pages_ref, send_ref):
    cached = dot(place_rows(row_key_ref[...]), pages_ref[...])
    send_ref[...] = (cached + fresh_ref[...].astype(F32)).astype(BF16)


def twiddles(cos_ref, sin_ref):
    c, s = cos_ref[...], sin_ref[...]
    half_c, half_s = c[:, 64:65], s[:, 64:65]
    step_c, step_s = half_c * half_c - half_s * half_s, 2.0 * half_c * half_s
    cosines, sines = [c], [s]
    for _ in range(3):
        c, s = c * step_c - s * step_s, c * step_s + s * step_c
        cosines.append(c)
        sines.append(s)
    return jnp.concatenate(cosines, axis=1), jnp.concatenate(sines, axis=1)


def forward(rows, first_ref, cosine, sine, high_ref, low_ref):
    part = dot(first_ref[...], rows)
    r = part[:N1] + part[2 * N1 : 3 * N1]
    i = part[N1 : 2 * N1] + part[3 * N1 :]
    br = r * cosine - i * sine
    bi = r * sine + i * cosine
    spectra = []
    for p, sign in enumerate((1.0, -1.0)):
        cr = br[:, :HALF] + sign * br[:, HALF:]
        ci = bi[:, :HALF] + sign * bi[:, HALF:]
        c = jnp.concatenate([cr, ci], axis=1).astype(BF16)
        spectra.append(dot(c, whole_table(high_ref[p])) + dot(c, whole_table(low_ref[p])))
    return spectra


def filter_kernel(*refs):
    keep_ref, came_ref, gain_ref, first_hbm, cos_ref, sin_ref, high_ref, low_ref, *refs = refs
    out_ref, first_ref, mine_ref, sems = refs
    copy = pltpu.make_async_copy(first_hbm, first_ref, sems)
    copy.start()
    _, _, core = place()
    col = lax.broadcasted_iota(jnp.int32, (1, N1), 1)
    key = ((col >> 3) & 15) * 16 + ((col >> 7) ^ core) * 8 + (col & 7)
    rows = reorder(key, jnp.concatenate([keep_ref[...], came_ref[...]], axis=0))
    lane = lax.broadcasted_iota(jnp.int32, (1, 32), 1)
    mine = jnp.where(lane == lax.axis_index("seq"), gain_ref[...], 0.0)
    mine_ref[...] = jnp.broadcast_to(jnp.sum(mine, axis=1, keepdims=True), (1, N2))
    cosine, sine = twiddles(cos_ref, sin_ref)
    copy.wait()
    spectra = forward(rows, first_ref, cosine, sine, high_ref, low_ref)
    for p, spec in enumerate(spectra):
        out_ref[p] = spec


def conv_kernel(x_ref, filter_ref, gain_ref, *refs):
    first_ref, cos_ref, sin_ref, high_ref, low_ref, last_hbm, out_ref, last_ref, sem = refs
    copy = pltpu.make_async_copy(last_hbm, last_ref, sem)
    copy.start()
    turned = []
    cosine, sine = twiddles(cos_ref, sin_ref)
    spectra = forward(x_ref[...], first_ref, cosine, sine, high_ref, low_ref)
    for p, spec in enumerate(spectra):
        xr, xi = spec[:, :HALF], spec[:, HALF:]
        hr, hi = filter_ref[p, :, :HALF], filter_ref[p, :, HALF:]
        prod = jnp.concatenate([xr * hr - xi * hi, xr * hi + xi * hr], axis=1).astype(BF16)
        turned.append(dot_t(prod, whole_table(high_ref[p])))
    plus = turned[0] + turned[1]
    minus = turned[0] - turned[1]
    dr = jnp.concatenate([plus[:, :HALF], minus[:, :HALF]], axis=1)
    di = jnp.concatenate([plus[:, HALF:], minus[:, HALF:]], axis=1)
    er = (dr * cosine + di * sine).astype(BF16)
    ei = (di * cosine - dr * sine).astype(BF16)
    copy.wait()
    convolved = dot(last_ref[...], jnp.concatenate([er, ei], axis=0))
    direct = gain_ref[...] * x_ref[...].astype(F32)
    out_ref[...] = (convolved + direct).astype(BF16)


def gate_kernel(total_ref, query_ref, out_ref):
    total = dot(place_rows(block_order()), total_ref[...])
    for a in range(8):
        cols = slice(a * N2, (a + 1) * N2)
        query = query_ref[:, cols].astype(F32)
        out_ref[:, cols] = (query * total[a * 32 : (a + 1) * 32, :]).astype(BF16)


def params():
    return pltpu.CompilerParams(vmem_limit_bytes=24 * 1024 * 1024)


def in_hbm(array):
    return pltpu.with_memory_space_constraint(array, pltpu.HBM)


def cost(flops, moved):
    return pl.CostEstimate(flops=flops, bytes_accessed=moved, transcendentals=0)


VMEM = pl.BlockSpec(memory_space=pltpu.VMEM)
ANY = pl.BlockSpec(memory_space=pl.ANY)
HBM = pl.BlockSpec(memory_space=pltpu.HBM)
SMEM = pl.BlockSpec(memory_space=pltpu.SMEM)


def hops(dx, dy, dcore):
    pairs = []
    for x in range(4):
        for y in range(4):
            for core in range(2):
                to = (((x + dx) % 4) * 4 + (y + dy) % 4) * 2 + (core + dcore) % 2
                pairs.append(((x * 4 + y) * 2 + core, to))
    return pairs


def shards(
    query_gate,
    key_stream,
    value_stream,
    filter_taps,
    skip_gain,
    page_pool,
    page_owner,
    page_slot,
    suffix_blocks,
):
    rows_of = lambda rows: jax.ShapeDtypeStruct((rows, N2), BF16)
    call = functools.partial(
        pl.pallas_call, compiler_params=params(), cost_estimate=cost(0, 1 << 20)
    )
    slabs, *along_y = call(
        slabs_kernel,
        out_shape=(pltpu.HBM((8, 2, 32, N2), BF16),) + (rows_of(64),) * 4,
        in_specs=[HBM, HBM],
        out_specs=(HBM,) + (VMEM,) * 4,
        scratch_shapes=[
            pltpu.VMEM((8, 2, 32, N2), BF16),
            pltpu.VMEM((32, 8 * N2), F32),
            pltpu.SemaphoreType.DMA((8,)),
            pltpu.SemaphoreType.DMA((8,)),
            pltpu.SemaphoreType.DMA,
        ],
        name="slabs",
    )(in_hbm(page_pool.reshape(8, 2, 32, N2)), in_hbm(filter_taps))
    pages = lax.all_to_all(
        slabs, "grp", split_axis=0, concat_axis=0, axis_index_groups=[RANKS], tiled=True
    ).reshape(512, N2)

    moved_y = [lax.ppermute(along_y[d], "seq", hops(0, d, 0)) for d in range(1, 4)]

    fresh, row_key = call(
        stage_kernel,
        out_shape=(rows_of(N1), jax.ShapeDtypeStruct((1, 512), jnp.int32)),
        in_specs=[HBM, HBM, SMEM, HBM, HBM, ANY],
        out_specs=(VMEM,) * 2,
        scratch_shapes=[
            pltpu.VMEM((1, 8), jnp.int32),
            pltpu.VMEM((1, 8), jnp.int32),
            pltpu.VMEM((32, 8 * N2), BF16),
            pltpu.VMEM((32, 8 * N2), BF16),
            pltpu.SemaphoreType.DMA((4,)),
        ],
        name="stage",
    )(
        in_hbm(page_owner),
        in_hbm(page_slot),
        suffix_blocks,
        in_hbm(key_stream[0]),
        in_hbm(value_stream[0]),
        along_y[0],
    )

    along_x = call(
        taps_x_kernel,
        out_shape=(rows_of(64),) * 4,
        in_specs=[VMEM] * 4 + [ANY],
        out_specs=(VMEM,) * 4,
        name="taps_x",
    )(along_y[0], *moved_y, row_key)
    moved_x = [lax.ppermute(along_x[d], "seq", hops(d, 0, 0)) for d in range(1, 4)]

    keep, other = call(
        taps_core_kernel,
        out_shape=(rows_of(128),) * 2,
        in_specs=[VMEM] * 4,
        out_specs=(VMEM,) * 2,
        cost_estimate=cost(1 << 34, 1 << 28),
        name="taps_core",
    )(along_x[0], *moved_x)
    came = lax.ppermute(other, "seq", hops(0, 0, 1))

    send = call(
        select_kernel,
        out_shape=rows_of(N1),
        in_specs=[VMEM] * 3,
        out_specs=VMEM,
        cost_estimate=cost(1 << 34, 1 << 28),
        name="select",
    )(row_key, fresh, pages)

    columns = lax.all_to_all(
        send.reshape(32, 8, N2), "seq", split_axis=0, concat_axis=0, tiled=True
    ).reshape(N1, N2)

    first, *middle, last = [jnp.asarray(t) for t in tables()]
    spectrum, first, gain = call(
        filter_kernel,
        out_shape=(
            jax.ShapeDtypeStruct((2, N1, N2), F32),
            jax.ShapeDtypeStruct(first.shape, BF16),
            jax.ShapeDtypeStruct((1, N2), F32),
        ),
        in_specs=[VMEM] * 3 + [HBM] + [VMEM] * 4,
        out_specs=(VMEM,) * 3,
        scratch_shapes=[pltpu.SemaphoreType.DMA],
        cost_estimate=cost(1 << 28, 1 << 28),
        name="filter",
    )(keep, came, skip_gain.reshape(1, 32), in_hbm(first), *middle)
    convolved = call(
        conv_kernel,
        out_shape=rows_of(N1),
        in_specs=[VMEM] * 8 + [HBM],
        out_specs=VMEM,
        scratch_shapes=[pltpu.VMEM((N1, N2), BF16), pltpu.SemaphoreType.DMA],
        cost_estimate=cost(0, 1 << 23),
        name="conv",
    )(columns, spectrum, gain, first, *middle, in_hbm(last))

    back = lax.all_to_all(
        convolved.reshape(32, 8, N2), "seq", split_axis=0, concat_axis=0, tiled=True
    ).reshape(N1, N2)

    gated = call(
        gate_kernel,
        out_shape=jax.ShapeDtypeStruct((32, 8 * N2), BF16),
        in_specs=[VMEM] * 2,
        out_specs=VMEM,
        name="gate",
    )(back, query_gate[0])
    return gated[None]


def solution(mesh):
    return jax.shard_map(
        shards,
        mesh=mesh,
        in_specs=(
            P("grp", None, "seq"),
            P("grp", None, "seq"),
            P("grp", None, "seq"),
            P(None, "seq"),
            P(),
            P("grp", "seq", None, None, None),
            P("grp", "seq"),
            P("grp", "seq"),
            P("grp"),
        ),
        out_specs=P("grp", None, "seq"),
        check_vma=False,
    )
```

```python
import functools

import jax
import jax.numpy as jnp
import ml_dtypes
import numpy as np
from jax import lax
from jax.experimental import pallas as pl
from jax.experimental.pallas import tpu as pltpu
from jax.sharding import PartitionSpec as P

N1 = 256
N2 = 512
HALF = N2 // 2
TOTAL = N1 * N2
RANKS = (4, 0, 5, 1, 6, 2, 7, 3)
STEP, UNSTEP = 13, 5
SEQ_RANKS = tuple(STEP * r % 32 for r in range(32))
BF16 = jnp.bfloat16
F32 = jnp.float32


@functools.cache
def tables():
    k1 = np.arange(N1)[:, None] + 0.25
    n1 = (np.array(SEQ_RANKS)[:, None] * 8 + np.arange(8)[None, :]).reshape(1, N1)
    rows = np.exp(-2j * np.pi * k1 * n1 / N1)
    first = np.concatenate([rows.real, rows.imag], axis=0)
    twiddle = np.exp(-2j * np.pi * k1 * np.arange(128)[None, :] / TOTAL)
    m = np.arange(HALF)[:, None]
    l = np.arange(HALF)[None, :]
    second = []
    for p in range(2):
        f = np.exp(-2j * np.pi * m * (l + 0.5 * p) / HALF)
        second.append(np.concatenate([f.real, f.imag], axis=1))
    back = rows.conj().T / TOTAL
    last = np.concatenate([back.real, -back.imag], axis=1)
    return (
        first.astype(ml_dtypes.bfloat16),
        twiddle.real.astype(np.float32),
        twiddle.imag.astype(np.float32),
        np.stack(second).astype(ml_dtypes.bfloat16),
        last.astype(ml_dtypes.bfloat16),
    )


def dot(a, b):
    return jnp.dot(a, b, preferred_element_type=F32)


def dot_t(a, b):
    return lax.dot_general(a, b, (((1,), (1,)), ((), ())), preferred_element_type=F32)


def whole_table(half):
    return jnp.concatenate(
        [half, jnp.concatenate([-half[:, HALF:], half[:, :HALF]], axis=1)], axis=0
    )


def place_rows(key_row):
    rows = lax.broadcasted_iota(jnp.int32, (N1, key_row.shape[1]), 0)
    return (rows == key_row).astype(F32).astype(BF16)


def send_order():
    col = lax.broadcasted_iota(jnp.int32, (1, N1), 1)
    return ((col * UNSTEP) & 31) * 8 + (col >> 5)


def block_order():
    col = lax.broadcasted_iota(jnp.int32, (1, N1), 1)
    return (col & 7) * 32 + (((col >> 3) * STEP) & 31)


def fetch(sources, targets, sems):
    copies = [
        pltpu.make_async_copy(source, target, sems.at[i])
        for i, (source, target) in enumerate(zip(sources, targets))
    ]
    for copy in copies:
        copy.start()
    for copy in copies:
        copy.wait()


def place():
    seq = lax.axis_index("seq")
    return seq >> 3, (seq >> 1) & 3, seq & 1


def reorder(key_row, rows):
    return dot(place_rows(key_row), rows).astype(BF16)


def slabs_kernel(pool_ref, taps_hbm, out_ref, *refs):
    outs, (held_ref, taps_ref, in_sems, out_sems, sem) = refs[:4], refs[4:]
    reads = [
        pltpu.make_async_copy(pool_ref.at[z], held_ref.at[r], in_sems.at[r])
        for r, z in enumerate(RANKS)
    ]
    writes = [
        pltpu.make_async_copy(held_ref.at[r], out_ref.at[r], out_sems.at[r]) for r in range(8)
    ]
    taps_read = pltpu.make_async_copy(taps_hbm, taps_ref, sem)
    for read in reads:
        read.start()
    taps_read.start()
    for read, write in zip(reads, writes):
        read.wait()
        write.start()
    taps_read.wait()
    _, y, _ = place()
    rows = jnp.concatenate([taps_ref[:, a * N2 : (a + 1) * N2] for a in range(8)], axis=0)
    col = lax.broadcasted_iota(jnp.int32, (1, N1), 1)
    step = (((col >> 1) & 3) - y) & 3
    key = step * 64 + ((col >> 3) & 3) * 16 + (col & 1) * 8 + (col >> 5)
    full = reorder(key, rows.astype(BF16))
    for d in range(4):
        outs[d][...] = full[d * 64 : (d + 1) * 64]
    for write in writes:
        write.wait()


def taps_x_kernel(*refs):
    ins, outs = refs[:4], refs[-4:]
    x, y, _ = place()
    col = lax.broadcasted_iota(jnp.int32, (1, N1), 1)
    step = (((col >> 4) & 3) - x) & 3
    key = step * 64 + ((col >> 3) & 1) * 32 + ((y - (col >> 6)) & 3) * 8 + (col & 7)
    full = reorder(key, jnp.concatenate([ref[...] for ref in ins], axis=0))
    for d in range(4):
        outs[d][...] = full[d * 64 : (d + 1) * 64]


def taps_core_kernel(*refs):
    ins, (keep_ref, send_ref) = refs[:4], refs[4:]
    x, _, core = place()
    col = lax.broadcasted_iota(jnp.int32, (1, N1), 1)
    other = ((col >> 5) & 1) ^ core
    key = other * 128 + ((x - (col >> 6)) & 3) * 32 + (col & 31)
    full = reorder(key, jnp.concatenate([ref[...] for ref in ins], axis=0))
    keep_ref[...] = full[:128]
    send_ref[...] = full[128:]


def stage_kernel(
    owner_hbm,
    slot_hbm,
    suffix_ref,
    key_hbm,
    value_hbm,
    tie_ref,
    fresh_ref,
    row_key_ref,
    owner_ref,
    slot_ref,
    key_ref,
    value_ref,
    sems,
):
    del tie_ref
    fetch(
        [owner_hbm, slot_hbm, key_hbm, value_hbm],
        [owner_ref, slot_ref, key_ref, value_ref],
        sems,
    )
    owner, slot = owner_ref[...], slot_ref[...]
    count = 256 - lax.axis_index("seq") * 8 - suffix_ref[0]
    column = lax.broadcasted_iota(jnp.int32, (1, 512), 1)
    row_key = jnp.full((1, 512), -1, jnp.int32)
    rank = sum(jnp.where(owner == z, r, 0) for r, z in enumerate(RANKS))
    page = rank * 2 + slot - lax.axis_index("grp") * 2
    fresh = []
    for a in range(8):
        hit = ((column >> 5) == page[:, a : a + 1]) & (count > a)
        row_key = jnp.where(hit, ((column * UNSTEP) & 31) * 8 + a, row_key)
        cols = slice(a * N2, (a + 1) * N2)
        product = key_ref[:, cols].astype(F32) * value_ref[:, cols].astype(F32)
        fresh.append(jnp.where(count > a, 0.0, product))
    row_key_ref[...] = row_key
    fresh_ref[...] = reorder(send_order(), jnp.concatenate(fresh, axis=0).astype(BF16))


def select_kernel(row_key_ref, fresh_ref, pages_ref, send_ref):
    cached = dot(place_rows(row_key_ref[...]), pages_ref[...])
    send_ref[...] = (cached + fresh_ref[...].astype(F32)).astype(BF16)


def twiddles(cos_ref, sin_ref):
    c, s = cos_ref[...], sin_ref[...]
    half_c, half_s = c[:, 64:65], s[:, 64:65]
    step_c, step_s = half_c * half_c - half_s * half_s, 2.0 * half_c * half_s
    cosines, sines = [c], [s]
    for _ in range(3):
        c, s = c * step_c - s * step_s, c * step_s + s * step_c
        cosines.append(c)
        sines.append(s)
    return jnp.concatenate(cosines, axis=1), jnp.concatenate(sines, axis=1)


def forward(rows, first_ref, cosine, sine, second_ref):
    part = dot(first_ref[...], rows)
    r, i = part[:N1], part[N1:]
    br = r * cosine - i * sine
    bi = r * sine + i * cosine
    spectra = []
    for p, sign in enumerate((1.0, -1.0)):
        cr = br[:, :HALF] + sign * br[:, HALF:]
        ci = bi[:, :HALF] + sign * bi[:, HALF:]
        c = jnp.concatenate([cr, ci], axis=1).astype(BF16)
        spectra.append(dot(c, whole_table(second_ref[p])))
    return spectra


def filter_kernel(*refs):
    keep_ref, came_ref, gain_ref, first_hbm, cos_ref, sin_ref, second_ref, *refs = refs
    out_ref, first_ref, mine_ref, sems = refs
    copy = pltpu.make_async_copy(first_hbm, first_ref, sems)
    copy.start()
    _, _, core = place()
    col = lax.broadcasted_iota(jnp.int32, (1, N1), 1)
    source = ((col >> 3) & 15) * 2 + ((col >> 7) ^ core)
    key = ((source * UNSTEP) & 31) * 8 + (col & 7)
    rows = reorder(key, jnp.concatenate([keep_ref[...], came_ref[...]], axis=0))
    lane = lax.broadcasted_iota(jnp.int32, (1, 32), 1)
    mine = jnp.where(lane == lax.axis_index("seq"), gain_ref[...], 0.0)
    mine_ref[...] = jnp.broadcast_to(jnp.sum(mine, axis=1, keepdims=True), (1, N2))
    cosine, sine = twiddles(cos_ref, sin_ref)
    copy.wait()
    spectra = forward(rows, first_ref, cosine, sine, second_ref)
    for p, spec in enumerate(spectra):
        out_ref[p] = spec


def conv_kernel(x_ref, filter_ref, gain_ref, *refs):
    first_ref, cos_ref, sin_ref, second_ref, last_hbm, out_ref, last_ref, sem = refs
    copy = pltpu.make_async_copy(last_hbm, last_ref, sem)
    copy.start()
    turned = []
    cosine, sine = twiddles(cos_ref, sin_ref)
    spectra = forward(x_ref[...], first_ref, cosine, sine, second_ref)
    for p, spec in enumerate(spectra):
        xr, xi = spec[:, :HALF], spec[:, HALF:]
        hr, hi = filter_ref[p, :, :HALF], filter_ref[p, :, HALF:]
        prod = jnp.concatenate([xr * hr - xi * hi, xr * hi + xi * hr], axis=1).astype(BF16)
        turned.append(dot_t(prod, whole_table(second_ref[p])))
    plus = turned[0] + turned[1]
    minus = turned[0] - turned[1]
    dr = jnp.concatenate([plus[:, :HALF], minus[:, :HALF]], axis=1)
    di = jnp.concatenate([plus[:, HALF:], minus[:, HALF:]], axis=1)
    er = (dr * cosine + di * sine).astype(BF16)
    ei = (di * cosine - dr * sine).astype(BF16)
    copy.wait()
    convolved = dot(last_ref[...], jnp.concatenate([er, ei], axis=0))
    direct = gain_ref[...] * x_ref[...].astype(F32)
    out_ref[...] = (convolved + direct).astype(BF16)


def gate_kernel(total_ref, query_ref, out_ref):
    total = dot(place_rows(block_order()), total_ref[...])
    for a in range(8):
        cols = slice(a * N2, (a + 1) * N2)
        query = query_ref[:, cols].astype(F32)
        out_ref[:, cols] = (query * total[a * 32 : (a + 1) * 32, :]).astype(BF16)


def params():
    return pltpu.CompilerParams(vmem_limit_bytes=24 * 1024 * 1024)


def in_hbm(array):
    return pltpu.with_memory_space_constraint(array, pltpu.HBM)


def cost(flops, moved):
    return pl.CostEstimate(flops=flops, bytes_accessed=moved, transcendentals=0)


VMEM = pl.BlockSpec(memory_space=pltpu.VMEM)
ANY = pl.BlockSpec(memory_space=pl.ANY)
HBM = pl.BlockSpec(memory_space=pltpu.HBM)
SMEM = pl.BlockSpec(memory_space=pltpu.SMEM)


def hops(dx, dy, dcore):
    pairs = []
    for x in range(4):
        for y in range(4):
            for core in range(2):
                to = (((x + dx) % 4) * 4 + (y + dy) % 4) * 2 + (core + dcore) % 2
                pairs.append(((x * 4 + y) * 2 + core, to))
    return pairs


def shards(
    query_gate,
    key_stream,
    value_stream,
    filter_taps,
    skip_gain,
    page_pool,
    page_owner,
    page_slot,
    suffix_blocks,
):
    rows_of = lambda rows: jax.ShapeDtypeStruct((rows, N2), BF16)
    call = functools.partial(
        pl.pallas_call, compiler_params=params(), cost_estimate=cost(0, 1 << 20)
    )
    slabs, *along_y = call(
        slabs_kernel,
        out_shape=(pltpu.HBM((8, 2, 32, N2), BF16),) + (rows_of(64),) * 4,
        in_specs=[HBM, HBM],
        out_specs=(HBM,) + (VMEM,) * 4,
        scratch_shapes=[
            pltpu.VMEM((8, 2, 32, N2), BF16),
            pltpu.VMEM((32, 8 * N2), F32),
            pltpu.SemaphoreType.DMA((8,)),
            pltpu.SemaphoreType.DMA((8,)),
            pltpu.SemaphoreType.DMA,
        ],
        name="slabs",
    )(in_hbm(page_pool.reshape(8, 2, 32, N2)), in_hbm(filter_taps))
    pages = lax.all_to_all(
        slabs, "grp", split_axis=0, concat_axis=0, axis_index_groups=[RANKS], tiled=True
    ).reshape(512, N2)

    moved_y = [lax.ppermute(along_y[d], "seq", hops(0, d, 0)) for d in range(1, 4)]

    fresh, row_key = call(
        stage_kernel,
        out_shape=(rows_of(N1), jax.ShapeDtypeStruct((1, 512), jnp.int32)),
        in_specs=[HBM, HBM, SMEM, HBM, HBM, ANY],
        out_specs=(VMEM,) * 2,
        scratch_shapes=[
            pltpu.VMEM((1, 8), jnp.int32),
            pltpu.VMEM((1, 8), jnp.int32),
            pltpu.VMEM((32, 8 * N2), BF16),
            pltpu.VMEM((32, 8 * N2), BF16),
            pltpu.SemaphoreType.DMA((4,)),
        ],
        name="stage",
    )(
        in_hbm(page_owner),
        in_hbm(page_slot),
        suffix_blocks,
        in_hbm(key_stream[0]),
        in_hbm(value_stream[0]),
        along_y[0],
    )

    along_x = call(
        taps_x_kernel,
        out_shape=(rows_of(64),) * 4,
        in_specs=[VMEM] * 4 + [ANY],
        out_specs=(VMEM,) * 4,
        name="taps_x",
    )(along_y[0], *moved_y, row_key)
    moved_x = [lax.ppermute(along_x[d], "seq", hops(d, 0, 0)) for d in range(1, 4)]

    keep, other = call(
        taps_core_kernel,
        out_shape=(rows_of(128),) * 2,
        in_specs=[VMEM] * 4,
        out_specs=(VMEM,) * 2,
        cost_estimate=cost(1 << 34, 1 << 28),
        name="taps_core",
    )(along_x[0], *moved_x)
    came = lax.ppermute(other, "seq", hops(0, 0, 1))

    send = call(
        select_kernel,
        out_shape=rows_of(N1),
        in_specs=[VMEM] * 3,
        out_specs=VMEM,
        cost_estimate=cost(1 << 34, 1 << 28),
        name="select",
    )(row_key, fresh, pages)

    columns = lax.all_to_all(
        send.reshape(32, 8, N2), "seq", split_axis=0, concat_axis=0, axis_index_groups=[SEQ_RANKS], tiled=True
    ).reshape(N1, N2)

    first, *middle, last = [jnp.asarray(t) for t in tables()]
    spectrum, first, gain = call(
        filter_kernel,
        out_shape=(
            jax.ShapeDtypeStruct((2, N1, N2), F32),
            jax.ShapeDtypeStruct(first.shape, BF16),
            jax.ShapeDtypeStruct((1, N2), F32),
        ),
        in_specs=[VMEM] * 3 + [HBM] + [VMEM] * 3,
        out_specs=(VMEM,) * 3,
        scratch_shapes=[pltpu.SemaphoreType.DMA],
        cost_estimate=cost(1 << 28, 1 << 28),
        name="filter",
    )(keep, came, skip_gain.reshape(1, 32), in_hbm(first), *middle)
    convolved = call(
        conv_kernel,
        out_shape=rows_of(N1),
        in_specs=[VMEM] * 7 + [HBM],
        out_specs=VMEM,
        scratch_shapes=[pltpu.VMEM((N1, N2), BF16), pltpu.SemaphoreType.DMA],
        cost_estimate=cost(0, 1 << 23),
        name="conv",
    )(columns, spectrum, gain, first, *middle, in_hbm(last))

    back = lax.all_to_all(
        convolved.reshape(32, 8, N2), "seq", split_axis=0, concat_axis=0, axis_index_groups=[SEQ_RANKS], tiled=True
    ).reshape(N1, N2)

    gated = call(
        gate_kernel,
        out_shape=jax.ShapeDtypeStruct((32, 8 * N2), BF16),
        in_specs=[VMEM] * 2,
        out_specs=VMEM,
        name="gate",
    )(back, query_gate[0])
    return gated[None]


def solution(mesh):
    return jax.shard_map(
        shards,
        mesh=mesh,
        in_specs=(
            P("grp", None, "seq"),
            P("grp", None, "seq"),
            P("grp", None, "seq"),
            P(None, "seq"),
            P(),
            P("grp", "seq", None, None, None),
            P("grp", "seq"),
            P("grp", "seq"),
            P("grp"),
        ),
        out_specs=P("grp", None, "seq"),
        check_vma=False,
    )
```

```python
import functools

import jax
import jax.numpy as jnp
import ml_dtypes
import numpy as np
from jax import lax
from jax.experimental import pallas as pl
from jax.experimental.pallas import tpu as pltpu
from jax.sharding import PartitionSpec as P

N1 = 256
N2 = 512
HALF = N2 // 2
TOTAL = N1 * N2
RANKS = (4, 0, 7, 1, 6, 2, 5, 3)
STEP, UNSTEP = 11, 3
SEQ_RANKS = tuple(STEP * r % 32 for r in range(32))
BF16 = jnp.bfloat16
F32 = jnp.float32


@functools.cache
def tables():
    k1 = np.arange(N1)[:, None] + 0.25
    n1 = (np.array(SEQ_RANKS)[:, None] * 8 + np.arange(8)[None, :]).reshape(1, N1)
    rows = np.exp(-2j * np.pi * k1 * n1 / N1)
    first = np.concatenate([rows.real, rows.imag], axis=0)
    twiddle = np.exp(-2j * np.pi * k1 * np.arange(128)[None, :] / TOTAL)
    m = np.arange(HALF)[:, None]
    l = np.arange(HALF)[None, :]
    second = []
    for p in range(2):
        f = np.exp(-2j * np.pi * m * (l + 0.5 * p) / HALF)
        second.append(np.concatenate([f.real, f.imag], axis=1))
    back = rows.conj().T / TOTAL
    last = np.concatenate([back.real, -back.imag], axis=1)
    return (
        first.astype(ml_dtypes.bfloat16),
        twiddle.real.astype(np.float32),
        twiddle.imag.astype(np.float32),
        np.stack(second).astype(ml_dtypes.bfloat16),
        last.astype(ml_dtypes.bfloat16),
    )


def dot(a, b):
    return jnp.dot(a, b, preferred_element_type=F32)


def dot_t(a, b):
    return lax.dot_general(a, b, (((1,), (1,)), ((), ())), preferred_element_type=F32)


def whole_table(half):
    return jnp.concatenate(
        [half, jnp.concatenate([-half[:, HALF:], half[:, :HALF]], axis=1)], axis=0
    )


def place_rows(key_row):
    rows = lax.broadcasted_iota(jnp.int32, (N1, key_row.shape[1]), 0)
    return (rows == key_row).astype(F32).astype(BF16)


def send_order():
    col = lax.broadcasted_iota(jnp.int32, (1, N1), 1)
    return ((col * UNSTEP) & 31) * 8 + (col >> 5)


def block_order():
    col = lax.broadcasted_iota(jnp.int32, (1, N1), 1)
    return (col & 7) * 32 + (((col >> 3) * STEP) & 31)


def fetch(sources, targets, sems):
    copies = [
        pltpu.make_async_copy(source, target, sems.at[i])
        for i, (source, target) in enumerate(zip(sources, targets))
    ]
    for copy in copies:
        copy.start()
    for copy in copies:
        copy.wait()


def place():
    seq = lax.axis_index("seq")
    return seq >> 3, (seq >> 1) & 3, seq & 1


def reorder(key_row, rows):
    return dot(place_rows(key_row), rows).astype(BF16)


def slabs_kernel(pool_ref, taps_hbm, out_ref, *refs):
    outs, (held_ref, taps_ref, in_sems, out_sems, sem) = refs[:4], refs[4:]
    reads = [
        pltpu.make_async_copy(pool_ref.at[z], held_ref.at[r], in_sems.at[r])
        for r, z in enumerate(RANKS)
    ]
    writes = [
        pltpu.make_async_copy(held_ref.at[r], out_ref.at[r], out_sems.at[r]) for r in range(8)
    ]
    taps_read = pltpu.make_async_copy(taps_hbm, taps_ref, sem)
    for read in reads:
        read.start()
    taps_read.start()
    for read, write in zip(reads, writes):
        read.wait()
        write.start()
    taps_read.wait()
    _, y, _ = place()
    rows = jnp.concatenate([taps_ref[:, a * N2 : (a + 1) * N2] for a in range(8)], axis=0)
    col = lax.broadcasted_iota(jnp.int32, (1, N1), 1)
    step = (((col >> 1) & 3) - y) & 3
    key = step * 64 + ((col >> 3) & 3) * 16 + (col & 1) * 8 + (col >> 5)
    full = reorder(key, rows.astype(BF16))
    for d in range(4):
        outs[d][...] = full[d * 64 : (d + 1) * 64]
    for write in writes:
        write.wait()


def taps_x_kernel(*refs):
    ins, outs = refs[:4], refs[-4:]
    x, y, _ = place()
    col = lax.broadcasted_iota(jnp.int32, (1, N1), 1)
    step = (((col >> 4) & 3) - x) & 3
    key = step * 64 + ((col >> 3) & 1) * 32 + ((y - (col >> 6)) & 3) * 8 + (col & 7)
    full = reorder(key, jnp.concatenate([ref[...] for ref in ins], axis=0))
    for d in range(4):
        outs[d][...] = full[d * 64 : (d + 1) * 64]


def taps_core_kernel(*refs):
    ins, (keep_ref, send_ref) = refs[:4], refs[4:]
    x, _, core = place()
    col = lax.broadcasted_iota(jnp.int32, (1, N1), 1)
    other = ((col >> 5) & 1) ^ core
    key = other * 128 + ((x - (col >> 6)) & 3) * 32 + (col & 31)
    full = reorder(key, jnp.concatenate([ref[...] for ref in ins], axis=0))
    keep_ref[...] = full[:128]
    send_ref[...] = full[128:]


def stage_kernel(
    owner_hbm,
    slot_hbm,
    suffix_ref,
    key_hbm,
    value_hbm,
    tie_ref,
    fresh_ref,
    row_key_ref,
    owner_ref,
    slot_ref,
    key_ref,
    value_ref,
    sems,
):
    del tie_ref
    fetch(
        [owner_hbm, slot_hbm, key_hbm, value_hbm],
        [owner_ref, slot_ref, key_ref, value_ref],
        sems,
    )
    owner, slot = owner_ref[...], slot_ref[...]
    count = 256 - lax.axis_index("seq") * 8 - suffix_ref[0]
    column = lax.broadcasted_iota(jnp.int32, (1, 512), 1)
    row_key = jnp.full((1, 512), -1, jnp.int32)
    rank = sum(jnp.where(owner == z, r, 0) for r, z in enumerate(RANKS))
    page = rank * 2 + slot - lax.axis_index("grp") * 2
    fresh = []
    for a in range(8):
        hit = ((column >> 5) == page[:, a : a + 1]) & (count > a)
        row_key = jnp.where(hit, ((column * UNSTEP) & 31) * 8 + a, row_key)
        cols = slice(a * N2, (a + 1) * N2)
        product = key_ref[:, cols].astype(F32) * value_ref[:, cols].astype(F32)
        fresh.append(jnp.where(count > a, 0.0, product))
    row_key_ref[...] = row_key
    fresh_ref[...] = reorder(send_order(), jnp.concatenate(fresh, axis=0).astype(BF16))


def select_kernel(row_key_ref, fresh_ref, pages_ref, send_ref):
    cached = dot(place_rows(row_key_ref[...]), pages_ref[...])
    send_ref[...] = (cached + fresh_ref[...].astype(F32)).astype(BF16)


def twiddles(cos_ref, sin_ref):
    c, s = cos_ref[...], sin_ref[...]
    half_c, half_s = c[:, 64:65], s[:, 64:65]
    step_c, step_s = half_c * half_c - half_s * half_s, 2.0 * half_c * half_s
    cosines, sines = [c], [s]
    for _ in range(3):
        c, s = c * step_c - s * step_s, c * step_s + s * step_c
        cosines.append(c)
        sines.append(s)
    return jnp.concatenate(cosines, axis=1), jnp.concatenate(sines, axis=1)


def forward(rows, first_ref, cosine, sine, second_ref):
    part = dot(first_ref[...], rows)
    r, i = part[:N1], part[N1:]
    br = r * cosine - i * sine
    bi = r * sine + i * cosine
    spectra = []
    for p, sign in enumerate((1.0, -1.0)):
        cr = br[:, :HALF] + sign * br[:, HALF:]
        ci = bi[:, :HALF] + sign * bi[:, HALF:]
        c = jnp.concatenate([cr, ci], axis=1).astype(BF16)
        spectra.append(dot(c, whole_table(second_ref[p])))
    return spectra


def filter_kernel(*refs):
    keep_ref, came_ref, gain_ref, first_hbm, cos_ref, sin_ref, second_ref, *refs = refs
    out_ref, first_ref, mine_ref, sems = refs
    copy = pltpu.make_async_copy(first_hbm, first_ref, sems)
    copy.start()
    _, _, core = place()
    col = lax.broadcasted_iota(jnp.int32, (1, N1), 1)
    source = ((col >> 3) & 15) * 2 + ((col >> 7) ^ core)
    key = ((source * UNSTEP) & 31) * 8 + (col & 7)
    rows = reorder(key, jnp.concatenate([keep_ref[...], came_ref[...]], axis=0))
    lane = lax.broadcasted_iota(jnp.int32, (1, 32), 1)
    mine = jnp.where(lane == lax.axis_index("seq"), gain_ref[...], 0.0)
    mine_ref[...] = jnp.broadcast_to(jnp.sum(mine, axis=1, keepdims=True), (1, N2))
    cosine, sine = twiddles(cos_ref, sin_ref)
    copy.wait()
    spectra = forward(rows, first_ref, cosine, sine, second_ref)
    for p, spec in enumerate(spectra):
        out_ref[p] = spec


def conv_kernel(x_ref, filter_ref, gain_ref, *refs):
    first_ref, cos_ref, sin_ref, second_ref, last_hbm, out_ref, last_ref, sem = refs
    copy = pltpu.make_async_copy(last_hbm, last_ref, sem)
    copy.start()
    turned = []
    cosine, sine = twiddles(cos_ref, sin_ref)
    spectra = forward(x_ref[...], first_ref, cosine, sine, second_ref)
    for p, spec in enumerate(spectra):
        xr, xi = spec[:, :HALF], spec[:, HALF:]
        hr, hi = filter_ref[p, :, :HALF], filter_ref[p, :, HALF:]
        prod = jnp.concatenate([xr * hr - xi * hi, xr * hi + xi * hr], axis=1).astype(BF16)
        turned.append(dot_t(prod, whole_table(second_ref[p])))
    plus = turned[0] + turned[1]
    minus = turned[0] - turned[1]
    dr = jnp.concatenate([plus[:, :HALF], minus[:, :HALF]], axis=1)
    di = jnp.concatenate([plus[:, HALF:], minus[:, HALF:]], axis=1)
    er = (dr * cosine + di * sine).astype(BF16)
    ei = (di * cosine - dr * sine).astype(BF16)
    copy.wait()
    convolved = dot(last_ref[...], jnp.concatenate([er, ei], axis=0))
    direct = gain_ref[...] * x_ref[...].astype(F32)
    out_ref[...] = (convolved + direct).astype(BF16)


def gate_kernel(total_ref, query_ref, out_ref):
    total = dot(place_rows(block_order()), total_ref[...])
    for a in range(8):
        cols = slice(a * N2, (a + 1) * N2)
        query = query_ref[:, cols].astype(F32)
        out_ref[:, cols] = (query * total[a * 32 : (a + 1) * 32, :]).astype(BF16)


def params():
    return pltpu.CompilerParams(vmem_limit_bytes=24 * 1024 * 1024)


def in_hbm(array):
    return pltpu.with_memory_space_constraint(array, pltpu.HBM)


def cost(flops, moved):
    return pl.CostEstimate(flops=flops, bytes_accessed=moved, transcendentals=0)


VMEM = pl.BlockSpec(memory_space=pltpu.VMEM)
ANY = pl.BlockSpec(memory_space=pl.ANY)
HBM = pl.BlockSpec(memory_space=pltpu.HBM)
SMEM = pl.BlockSpec(memory_space=pltpu.SMEM)


def hops(dx, dy, dcore):
    pairs = []
    for x in range(4):
        for y in range(4):
            for core in range(2):
                to = (((x + dx) % 4) * 4 + (y + dy) % 4) * 2 + (core + dcore) % 2
                pairs.append(((x * 4 + y) * 2 + core, to))
    return pairs


def shards(
    query_gate,
    key_stream,
    value_stream,
    filter_taps,
    skip_gain,
    page_pool,
    page_owner,
    page_slot,
    suffix_blocks,
):
    rows_of = lambda rows: jax.ShapeDtypeStruct((rows, N2), BF16)
    call = functools.partial(
        pl.pallas_call, compiler_params=params(), cost_estimate=cost(0, 1 << 20)
    )
    slabs, *along_y = call(
        slabs_kernel,
        out_shape=(pltpu.HBM((8, 2, 32, N2), BF16),) + (rows_of(64),) * 4,
        in_specs=[HBM, HBM],
        out_specs=(HBM,) + (VMEM,) * 4,
        scratch_shapes=[
            pltpu.VMEM((8, 2, 32, N2), BF16),
            pltpu.VMEM((32, 8 * N2), F32),
            pltpu.SemaphoreType.DMA((8,)),
            pltpu.SemaphoreType.DMA((8,)),
            pltpu.SemaphoreType.DMA,
        ],
        name="slabs",
    )(in_hbm(page_pool.reshape(8, 2, 32, N2)), in_hbm(filter_taps))
    pages = lax.all_to_all(
        slabs, "grp", split_axis=0, concat_axis=0, axis_index_groups=[RANKS], tiled=True
    ).reshape(512, N2)

    moved_y = [lax.ppermute(along_y[d], "seq", hops(0, d, 0)) for d in range(1, 4)]

    fresh, row_key = call(
        stage_kernel,
        out_shape=(rows_of(N1), jax.ShapeDtypeStruct((1, 512), jnp.int32)),
        in_specs=[HBM, HBM, SMEM, HBM, HBM, ANY],
        out_specs=(VMEM,) * 2,
        scratch_shapes=[
            pltpu.VMEM((1, 8), jnp.int32),
            pltpu.VMEM((1, 8), jnp.int32),
            pltpu.VMEM((32, 8 * N2), BF16),
            pltpu.VMEM((32, 8 * N2), BF16),
            pltpu.SemaphoreType.DMA((4,)),
        ],
        name="stage",
    )(
        in_hbm(page_owner),
        in_hbm(page_slot),
        suffix_blocks,
        in_hbm(key_stream[0]),
        in_hbm(value_stream[0]),
        along_y[0],
    )

    along_x = call(
        taps_x_kernel,
        out_shape=(rows_of(64),) * 4,
        in_specs=[VMEM] * 4 + [ANY],
        out_specs=(VMEM,) * 4,
        name="taps_x",
    )(along_y[0], *moved_y, row_key)
    moved_x = [lax.ppermute(along_x[d], "seq", hops(d, 0, 0)) for d in range(1, 4)]

    keep, other = call(
        taps_core_kernel,
        out_shape=(rows_of(128),) * 2,
        in_specs=[VMEM] * 4,
        out_specs=(VMEM,) * 2,
        cost_estimate=cost(1 << 34, 1 << 28),
        name="taps_core",
    )(along_x[0], *moved_x)
    came = lax.ppermute(other, "seq", hops(0, 0, 1))

    send = call(
        select_kernel,
        out_shape=rows_of(N1),
        in_specs=[VMEM] * 3,
        out_specs=VMEM,
        cost_estimate=cost(1 << 34, 1 << 28),
        name="select",
    )(row_key, fresh, pages)

    columns = lax.all_to_all(
        send.reshape(32, 8, N2), "seq", split_axis=0, concat_axis=0, axis_index_groups=[SEQ_RANKS], tiled=True
    ).reshape(N1, N2)

    first, *middle, last = [jnp.asarray(t) for t in tables()]
    spectrum, first, gain = call(
        filter_kernel,
        out_shape=(
            jax.ShapeDtypeStruct((2, N1, N2), F32),
            jax.ShapeDtypeStruct(first.shape, BF16),
            jax.ShapeDtypeStruct((1, N2), F32),
        ),
        in_specs=[VMEM] * 3 + [HBM] + [VMEM] * 3,
        out_specs=(VMEM,) * 3,
        scratch_shapes=[pltpu.SemaphoreType.DMA],
        cost_estimate=cost(1 << 28, 1 << 28),
        name="filter",
    )(keep, came, skip_gain.reshape(1, 32), in_hbm(first), *middle)
    convolved = call(
        conv_kernel,
        out_shape=rows_of(N1),
        in_specs=[VMEM] * 7 + [HBM],
        out_specs=VMEM,
        scratch_shapes=[pltpu.VMEM((N1, N2), BF16), pltpu.SemaphoreType.DMA],
        cost_estimate=cost(0, 1 << 23),
        name="conv",
    )(columns, spectrum, gain, first, *middle, in_hbm(last))

    back = lax.all_to_all(
        convolved.reshape(32, 8, N2), "seq", split_axis=0, concat_axis=0, axis_index_groups=[SEQ_RANKS], tiled=True
    ).reshape(N1, N2)

    gated = call(
        gate_kernel,
        out_shape=jax.ShapeDtypeStruct((32, 8 * N2), BF16),
        in_specs=[VMEM] * 2,
        out_specs=VMEM,
        name="gate",
    )(back, query_gate[0])
    return gated[None]


def solution(mesh):
    return jax.shard_map(
        shards,
        mesh=mesh,
        in_specs=(
            P("grp", None, "seq"),
            P("grp", None, "seq"),
            P("grp", None, "seq"),
            P(None, "seq"),
            P(),
            P("grp", "seq", None, None, None),
            P("grp", "seq"),
            P("grp", "seq"),
            P("grp"),
        ),
        out_specs=P("grp", None, "seq"),
        check_vma=False,
    )
```
